32 devices in a mesh: elem: 8 (over z, x), grp: 4 (over y, core).
Axes of the slice: x: 2, y: 2, z: 4, core: 2. Of those that a mesh axis runs over, the one named last changes fastest.
Arguments:
- state: float32 [256, 6, 512], P(('elem', 'grp')), may hold values from -6 to 20, as said below
- material: int32 [256], P(('elem', 'grp')), may hold values from 0 to 1
- metric: float32 [256], P(('elem', 'grp')), may hold values from 1 to 4
- mortar_proj: float32 [4, 64, 64], replicated, may hold values from 0 to 1, as said below
- mortar_map: int32 [32, 4, 96], P(('elem', 'grp')), may hold values from 0 to 7, as said below
- mortar_count: int32 [32, 6], P(('elem', 'grp')), may hold values from 0 to 32, as said below
- neighbours: int32 [256, 6], P(('elem', 'grp')), may hold values from -1 to 7, as said below
Outputs:
- new_state: float32 [256, 6, 512], P(('elem', 'grp'))
The draws below stay inside these ranges and needn't reach their ends.
Inputs may be any that keep to these rules, and one draw needn't show every extreme that they name: `state`: density and pressure, with either heat ratio, are positive at every node. `mortar_proj`: entries are nonnegative and every row sums to one. `mortar_map`: Rows: local element, face (0 to 5), subface (0 conforming, 1 to 4 a quadrant of a coarse face), orientation (0 to 7). Slot s below 32 pairs with slot (own grp index) * 8 + s % 8 of the device with the same elem index and grp index s // 8; the next 32 slots pair, position by position, with the last 32 slots of the device one elem index higher, the last 32 with the middle 32 of the device one elem index lower, same grp index. Paired faces lie along one dimension with opposite normals; at most one side of a pair has a nonzero subface. `mortar_count`: entry g below 4 counts the live slots toward grp peer g, 0 for the device itself, equal to the peer's entry for this device, at most 8 and reaching it on some devices; entry 4 toward the next elem index equals that device's entry 5; the top elem index has 0 in entry 4, the bottom one 0 in entry 5. Slots at positions below the count are live. `neighbours`: local element across the face, meeting its opposite face, or -1.
All inputs are finite; a program needn't handle non-finite values.
Results may differ from the reference program's by a relative error of at most 0.0003.
Values sent between devices are 32-bit elements; how exact they have to be, the bound alone decides.
A program may use at most 64 MiB of HBM per device.

```python
import math
import jax
import jax.numpy as jnp
import numpy as np
from jax import lax

NV = 6
NP = 8
FN = 64
VN = 512
SUBS = 4
EL_DEV = 8
CAPG = 8
CAPS = 32
SLOTS = 96
ELEMS = 256
N_ELEM = 8
N_GRP = 4
DEVICES = 32


def draw_state(key, part):
    keys = jax.random.split(key, 4)
    density = jnp.exp(jax.random.uniform(keys[0], (ELEMS, VN), jnp.float32, math.log(0.5), math.log(2.0)))
    velocity = jnp.clip(0.5 * jax.random.normal(keys[1], (ELEMS, 3, VN), jnp.float32), -2.0, 2.0)
    pressure = jnp.exp(jax.random.uniform(keys[2], (ELEMS, VN), jnp.float32, math.log(0.5), math.log(2.0)))
    scalar = jax.random.uniform(keys[3], (ELEMS, VN), jnp.float32)
    energy = pressure / 0.4 + 0.5 * density * jnp.sum(velocity * velocity, axis=1)
    return jnp.concatenate([density[:, None], density[:, None] * velocity, energy[:, None], (density * scalar)[:, None]], axis=1)


def draw_mortar_proj(key, part):
    spread = jax.random.uniform(key, (SUBS, FN, FN), jnp.float32)
    spread = spread / jnp.sum(spread, axis=2, keepdims=True)
    return 0.6 * jnp.eye(FN, dtype=jnp.float32)[None] + 0.4 * spread


def link_tables(key):
    base = jax.random.fold_in(key, 7331)
    keys = jax.random.split(base, 8)
    grp_shape = (N_ELEM, N_GRP, N_GRP, CAPG)
    up_shape = (N_ELEM, N_GRP, CAPS)
    grp_code = jax.random.randint(keys[0], grp_shape, 0, 6, jnp.int32)
    grp_kind = jax.random.randint(keys[1], grp_shape, 0, 3, jnp.int32)
    grp_sub = jax.random.randint(keys[2], grp_shape, 1, 5, jnp.int32)
    grp_level = jax.random.randint(keys[3], (N_ELEM, N_GRP, N_GRP), 0, 4, jnp.int32)
    up_code = jax.random.randint(keys[4], up_shape, 0, 6, jnp.int32)
    up_kind = jax.random.randint(keys[5], up_shape, 0, 3, jnp.int32)
    up_sub = jax.random.randint(keys[6], up_shape, 1, 5, jnp.int32)
    up_level = jax.random.randint(keys[7], (N_ELEM, N_GRP), 0, 4, jnp.int32)
    return (grp_code, grp_kind, grp_sub, grp_level, up_code, up_kind, up_sub, up_level)


def draw_mortar_count(key, part):
    grp_code, grp_kind, grp_sub, grp_level, up_code, up_kind, up_sub, up_level = link_tables(key)
    order = jnp.arange(N_GRP, dtype=jnp.int32)
    low_index = jnp.minimum(order[:, None], order[None, :])
    high_index = jnp.maximum(order[:, None], order[None, :])
    level = grp_level[:, low_index, high_index]
    pinned = (low_index == 0) & (high_index == 1)
    level = jnp.where(pinned[None], 0, level)
    grp_count = CAPG * jnp.right_shift(jnp.int32(8), level) // 8
    grp_count = jnp.where((order[:, None] == order[None, :])[None], 0, grp_count)
    elem_order = jnp.arange(N_ELEM, dtype=jnp.int32)
    first = (elem_order[:, None] == 0) & (order[None, :] == 0)
    link_level = jnp.where(first, 0, up_level)
    link = CAPS * jnp.right_shift(jnp.int32(8), link_level) // 8
    link = jnp.where((elem_order == N_ELEM - 1)[:, None], 0, link)
    below = jnp.concatenate([jnp.zeros((1, N_GRP), jnp.int32), link[:-1]], axis=0)
    table = jnp.concatenate([grp_count, link[:, :, None], below[:, :, None]], axis=2)
    return table.reshape(DEVICES, N_GRP + 2).astype(jnp.int32)


def draw_mortar_map(key, part):
    grp_code, grp_kind, grp_sub, grp_level, up_code, up_kind, up_sub, up_level = link_tables(key)
    order = jnp.arange(N_GRP, dtype=jnp.int32)
    low_index = jnp.minimum(order[:, None], order[None, :])
    high_index = jnp.maximum(order[:, None], order[None, :])
    code = grp_code[:, low_index, high_index]
    kind = grp_kind[:, low_index, high_index]
    quadrant = grp_sub[:, low_index, high_index]
    is_lower = (order[:, None] < order[None, :])[None, :, :, None]
    grp_face = jnp.where(is_lower, code, jnp.bitwise_xor(code, 1)).reshape(N_ELEM, N_GRP, N_GRP * CAPG)
    grp_subs = jnp.where(is_lower & (kind == 1) | jnp.logical_not(is_lower) & (kind == 2), quadrant, 0).reshape(N_ELEM, N_GRP, N_GRP * CAPG)
    up_face = up_code
    up_subs = jnp.where(up_kind == 1, up_sub, 0)
    code_below = jnp.concatenate([jnp.zeros_like(up_code[:1]), up_code[:-1]], axis=0)
    kind_below = jnp.concatenate([jnp.zeros_like(up_kind[:1]), up_kind[:-1]], axis=0)
    sub_below = jnp.concatenate([jnp.zeros_like(up_sub[:1]), up_sub[:-1]], axis=0)
    down_face = jnp.bitwise_xor(code_below, 1)
    down_subs = jnp.where(kind_below == 2, sub_below, 0)
    face = jnp.concatenate([grp_face, up_face, down_face], axis=2)
    subface = jnp.concatenate([grp_subs, up_subs, down_subs], axis=2)
    element = jax.random.randint(jax.random.fold_in(key, 11), (N_ELEM, N_GRP, SLOTS), 0, EL_DEV, jnp.int32)
    orient = jax.random.randint(jax.random.fold_in(key, 13), (N_ELEM, N_GRP, SLOTS), 0, 8, jnp.int32)
    stacked = jnp.stack([element, face, subface, orient], axis=2)
    return stacked.reshape(DEVICES, 4, SLOTS).astype(jnp.int32)


def draw_neighbours(key, part):
    keys = jax.random.split(jax.random.fold_in(key, 17), 2)
    target = jax.random.randint(keys[0], (ELEMS, 6), 0, EL_DEV, jnp.int32)
    keep = jax.random.randint(keys[1], (ELEMS, 6), 0, 2, jnp.int32)
    return jnp.where(keep == 1, target, -1).astype(jnp.int32)


def plant(values, key, smallest, top_value):
    index_at = [jax.random.randint(jax.random.fold_in(key, axis), (), 0, length) for axis, length in enumerate(values.shape)]
    main_axis = values.shape.index(max(values.shape))
    neighbour = index_at[:main_axis] + [(index_at[main_axis] + 1) % values.shape[main_axis]] + index_at[main_axis + 1:]
    return values.at[tuple(index_at)].set(smallest).at[tuple(neighbour)].set(top_value)


def levels(own_key, dims, cuts, smallest, top_value):
    def one(axis_at, blocks):
        steps = jax.random.uniform(jax.random.fold_in(jax.random.fold_in(own_key, 6), axis_at), (blocks,), jnp.float32, smallest / len(cuts), top_value / len(cuts))
        return jnp.repeat(jnp.exp(steps), dims[axis_at] // blocks).reshape((-1,) + (1,) * (len(dims) - axis_at - 1))

    level = one(*cuts[0])
    for cut in cuts[1:]:
        level = level * one(*cut)
    return level


def setup_inputs(seed: int = 0) -> dict:
    splits = jax.random.split(jax.random.key(seed), 8)
    return {
        "state": draw_state(jax.random.fold_in(splits[7], 71), 0),
        "material": plant(jax.random.randint(splits[1], (ELEMS,), 0, 2), jax.random.fold_in(splits[1], 1), 0, 1).astype(jnp.int32),
        "metric": jnp.clip(jnp.exp(math.log(4.0) - 1.3862944 * jax.random.uniform(splits[2], (ELEMS,), jnp.float32) ** levels(splits[2], (ELEMS,), ((0, 32),), -0.2, 0.2)), 1.0, 4.0),
        "mortar_proj": draw_mortar_proj(jax.random.fold_in(splits[7], 71), 0),
        "mortar_map": draw_mortar_map(jax.random.fold_in(splits[7], 71), 0),
        "mortar_count": draw_mortar_count(jax.random.fold_in(splits[7], 71), 0),
        "neighbours": draw_neighbours(jax.random.fold_in(splits[7], 71), 0),
    }


highest = lax.Precision.HIGHEST
step_size = 0.002
lift_weight = 49.0

def cheb_matrix():
    points = -np.cos(np.pi * np.arange(8) / 7.0)
    factor = np.array([2.0, 1.0, 1.0, 1.0, 1.0, 1.0, 1.0, 2.0])
    alternating = np.where(np.arange(8) % 2 == 0, 1.0, -1.0)
    scaled = factor * alternating
    differ = points[:, None] - points[None, :] + np.eye(8)
    matrix = scaled[:, None] / scaled[None, :] / differ
    matrix = matrix * (1.0 - np.eye(8))
    return matrix - np.eye(8) * matrix.sum(axis=1)[:, None]

def face_plane(node_grid, face):
    index = 0 if face % 2 == 0 else 7
    if face // 2 == 0:
        return node_grid[index]
    if face // 2 == 1:
        return node_grid[:, index]
    return node_grid[:, :, index]

def face_select():
    node_grid = np.arange(512).reshape(8, 8, 8)
    layers = []
    for face in range(6):
        layers.append(face_plane(node_grid, face).reshape(64))
    nodes = np.concatenate(layers)
    return (nodes[:, None] == np.arange(512)[None, :]).astype(np.float32)

def orient_matrices():
    first, second = np.meshgrid(np.arange(8), np.arange(8), indexing='ij')
    result = []
    for orient in range(8):
        row_p, row_r = (second, first) if orient & 4 else (first, second)
        if orient & 1:
            row_p = 7 - row_p
        if orient & 2:
            row_r = 7 - row_r
        source = (8 * row_p + row_r).reshape(64)
        result.append((source[:, None] == np.arange(64)[None, :]).astype(np.float32))
    return np.stack(result)

def state_parts(cons, heat_ratio, normal):
    density = cons[:, 0]
    momentum = cons[:, 1:4]
    energy = cons[:, 4]
    scalar = cons[:, 5]
    velocity = momentum / density[:, None]
    pressure = (heat_ratio[:, None] - 1.0) * (energy - 0.5 * lax.optimization_barrier(jnp.sum(momentum * velocity, axis=1)))
    direction = normal[:, :, None]
    speed_n = lax.optimization_barrier(jnp.sum(direction * velocity, axis=1))
    sound_speed = jnp.sqrt(heat_ratio[:, None] * pressure / density)
    phys_flux = jnp.concatenate([(density * speed_n)[:, None], momentum * speed_n[:, None] + pressure[:, None] * direction, ((energy + pressure) * speed_n)[:, None], (scalar * speed_n)[:, None]], axis=1)
    return (density, velocity, pressure, speed_n, sound_speed, energy, scalar, phys_flux)

def star_state(parts, wave_speed, middle, normal):
    density, velocity, pressure, speed_n, sound_speed, energy, scalar, phys_flux = parts
    relative = wave_speed - speed_n
    factor = density * relative / (wave_speed - middle)
    shifted = middle - speed_n
    momentum = factor[:, None] * (velocity + shifted[:, None] * normal[:, :, None])
    energy_star = factor * (energy / density + shifted * (middle + pressure / (density * relative)))
    return jnp.concatenate([factor[:, None], momentum, energy_star[:, None], (factor * scalar / density)[:, None]], axis=1)

def hllc_flux(left, right, heat_left, heat_right, normal):
    left_parts = state_parts(left, heat_left, normal)
    right_parts = state_parts(right, heat_right, normal)
    left_wave = jnp.minimum(left_parts[3] - left_parts[4], right_parts[3] - right_parts[4])
    right_wave = jnp.maximum(left_parts[3] + left_parts[4], right_parts[3] + right_parts[4])
    left_mass = left_parts[0] * (left_wave - left_parts[3])
    right_mass = right_parts[0] * (right_wave - right_parts[3])
    middle = (right_parts[2] - left_parts[2] + left_mass * left_parts[3] - right_mass * right_parts[3]) / (left_mass - right_mass)
    left_star = left_parts[7] + left_wave[:, None] * (star_state(left_parts, left_wave, middle, normal) - left)
    right_star = right_parts[7] + right_wave[:, None] * (star_state(right_parts, right_wave, middle, normal) - right)
    return jnp.where((left_wave >= 0.0)[:, None], left_parts[7], jnp.where((middle >= 0.0)[:, None], left_star, jnp.where((right_wave > 0.0)[:, None], right_star, right_parts[7])))

def normals_of(face):
    axis_id = face // 2
    orient_sign = jnp.where(face % 2 == 1, 1.0, -1.0).astype(jnp.float32)
    return orient_sign[:, None] * (axis_id[:, None] == jnp.arange(3, dtype=jnp.int32)[None, :]).astype(jnp.float32)

def face_traces(elements, select):
    count_el = elements.shape[0]
    flat_state = elements.reshape(count_el * NV, VN)
    traces = jnp.dot(flat_state, select.T, precision=highest, preferred_element_type=jnp.float32)
    return traces.reshape(count_el, NV, 6, FN).transpose(0, 2, 1, 3).reshape(count_el * 6, NV, FN)

def slot_operators(mortar_proj, mortar_info):
    identity = jnp.eye(FN, dtype=jnp.float32)
    proj_table = jnp.concatenate([identity[None], mortar_proj], axis=0)
    orients = jnp.asarray(orient_matrices(), jnp.float32)
    combos = jnp.einsum('spq,oqr->sopr', proj_table, orients, precision=highest).reshape((SUBS + 1) * 8, FN, FN)
    return combos[mortar_info[2] * 8 + mortar_info[3]]

def mortar_traces(face_rows, operators, heat_ratio, mortar_info):
    picked = face_rows[mortar_info[0] * 6 + mortar_info[1]]
    native = jnp.einsum('spq,svq->svp', operators, picked, precision=highest)
    return (native, heat_ratio[mortar_info[0]])

def slot_layout(groups, grp_index, counts):
    grp_slots = groups * CAPG
    slot_index = jnp.arange(grp_slots + 2 * CAPS, dtype=jnp.int32)
    peer_index = slot_index // CAPG
    in_grp = slot_index < grp_slots
    in_up = (slot_index >= grp_slots) & (slot_index < grp_slots + CAPS)
    group_id = jnp.where(in_grp, peer_index, jnp.where(in_up, groups, groups + 1))
    position = jnp.where(in_grp, slot_index % CAPG, (slot_index - grp_slots) % CAPS)
    slot_limit = lax.optimization_barrier(jnp.sum(jnp.where(group_id[:, None] == jnp.arange(groups + 2, dtype=jnp.int32)[None, :], counts[None, :], 0), axis=1))
    is_live = position < slot_limit
    is_lower = jnp.where(in_grp, grp_index < peer_index, in_up)
    return (is_lower, is_live)

def mortar_flux(native, partner, native_heat, partner_heat, normal, is_lower, is_live):
    live_mask = is_live[:, None, None]
    partner = jnp.where(live_mask, partner, native)
    partner_heat = jnp.where(is_live, partner_heat, native_heat)
    lower_mask = is_lower[:, None, None]
    low_side = jnp.where(lower_mask, native, partner)
    high_side = jnp.where(lower_mask, partner, native)
    low_heat = jnp.where(is_lower, native_heat, partner_heat)
    high_heat = jnp.where(is_lower, partner_heat, native_heat)
    low_normal = jnp.where(is_lower[:, None], normal, -normal)
    return hllc_flux(low_side, high_side, low_heat, high_heat, low_normal)

def volume_fluxes(elements, heat_ratio):
    fluxes = []
    for axis_id in range(3):
        direction = jnp.eye(3, dtype=jnp.float32)[axis_id][None, :]
        fluxes.append(state_parts(elements, heat_ratio, direction)[7])
    return fluxes

def volume_term(elements, heat_ratio):
    count_el = elements.shape[0]
    deriv = jnp.asarray(cheb_matrix(), jnp.float32)
    flux_x, flux_y, flux_z = [item.reshape(count_el, NV, NP, NP, NP) for item in volume_fluxes(elements, heat_ratio)]
    total = jnp.einsum('ia,evabc->evibc', deriv, flux_x, precision=highest)
    total = total + jnp.einsum('jb,evabc->evajc', deriv, flux_y, precision=highest)
    total = total + jnp.einsum('kc,evabc->evabk', deriv, flux_z, precision=highest)
    return -total.reshape(count_el, NV, VN)

def section_update(elements, heat_ratio, metric, mortar_info, neighbours, face_rows, operators, native, native_heat, flux_own, is_live, select, volume):
    count_el = elements.shape[0]
    normal = normals_of(mortar_info[1])
    correction = state_parts(native, native_heat, normal)[7] - flux_own
    correction = jnp.where(is_live[:, None, None], correction, 0.0)
    back_weight = jnp.where(mortar_info[2] == 0, 1.0, 0.25).astype(jnp.float32)
    projected = back_weight[:, None, None] * jnp.einsum('spq,svp->svq', operators, correction, precision=highest)
    face_id = jnp.tile(jnp.arange(6, dtype=jnp.int32), count_el)
    face_owner = jnp.repeat(jnp.arange(count_el, dtype=jnp.int32), 6)
    face_normal = normals_of(face_id)
    across = neighbours.reshape(count_el * 6)
    has_across = across >= 0
    safe_across = jnp.where(has_across, across, face_owner)
    source = jnp.where(has_across, across * 6 + jnp.bitwise_xor(face_id, 1), jnp.arange(count_el * 6, dtype=jnp.int32))
    partner = face_rows[source]
    row_heat = heat_ratio[face_owner]
    local_term = state_parts(face_rows, row_heat, face_normal)[7] - hllc_flux(face_rows, partner, row_heat, heat_ratio[safe_across], face_normal)
    local_term = jnp.where(has_across[:, None, None], local_term, 0.0)
    face_sum = local_term + jax.ops.segment_sum(projected, mortar_info[0] * 6 + mortar_info[1], num_segments=count_el * 6)
    placed = face_sum.reshape(count_el, 6, NV, FN).transpose(0, 2, 1, 3).reshape(count_el * NV, 6 * FN)
    surface = jnp.dot(placed, select, precision=highest, preferred_element_type=jnp.float32).reshape(count_el, NV, VN)
    return elements + step_size * metric[:, None, None] * (volume + lift_weight * surface)

def partner_slots(values):
    rest = values.shape[2:]
    grid = values.reshape((N_ELEM, N_GRP, SLOTS) + rest)
    grp_slots = N_GRP * CAPG
    grouped = grid[:, :, :grp_slots].reshape((N_ELEM, N_GRP, N_GRP, CAPG) + rest)
    swapped = jnp.swapaxes(grouped, 1, 2).reshape((N_ELEM, N_GRP, grp_slots) + rest)
    upward = grid[:, :, grp_slots:grp_slots + CAPS]
    downward = grid[:, :, grp_slots + CAPS:]
    above = jnp.concatenate([downward[1:], jnp.zeros_like(downward[:1])], axis=0)
    below = jnp.concatenate([jnp.zeros_like(upward[:1]), upward[:-1]], axis=0)
    return jnp.concatenate([swapped, above, below], axis=2).reshape((DEVICES, SLOTS) + rest)

def reference(state, material, metric, mortar_proj, mortar_map, mortar_count, neighbours):
    select = jnp.asarray(face_select(), jnp.float32)
    blocks = state.reshape(DEVICES, EL_DEV, NV, VN)
    materials = material.reshape(DEVICES, EL_DEV)
    metrics = metric.reshape(DEVICES, EL_DEV)
    across_all = neighbours.reshape(DEVICES, EL_DEV, 6)

    def first_pass(inputs):
        elements, kinds, mortar_info = inputs
        heat_ratio = 1.4 + 0.27 * kinds.astype(jnp.float32)
        face_rows = face_traces(elements, select)
        operators = slot_operators(mortar_proj, mortar_info)
        return mortar_traces(face_rows, operators, heat_ratio, mortar_info)
    natives, native_heats = lax.map(first_pass, (blocks, materials, mortar_map))
    partners = partner_slots(natives)
    partner_heats = partner_slots(native_heats)

    def second_pass(inputs):
        elements, kinds, scale, mortar_info, counts, across, native, native_heat, partner, partner_heat, device = inputs
        heat_ratio = 1.4 + 0.27 * kinds.astype(jnp.float32)
        face_rows = face_traces(elements, select)
        operators = slot_operators(mortar_proj, mortar_info)
        is_lower, is_live = slot_layout(N_GRP, device % N_GRP, counts)
        normal = normals_of(mortar_info[1])
        star_flux = mortar_flux(native, partner, native_heat, partner_heat, normal, is_lower, is_live)
        flux_own = jnp.where(is_lower[:, None, None], star_flux, -star_flux)
        volume = volume_term(elements, heat_ratio)
        return section_update(elements, heat_ratio, scale, mortar_info, across, face_rows, operators, native, native_heat, flux_own, is_live, select, volume)
    result = lax.map(second_pass, (blocks, materials, metrics, mortar_map, mortar_count, across_all, natives, native_heats, partners, partner_heats, jnp.arange(DEVICES, dtype=jnp.int32)))
    return result.reshape(ELEMS, NV, VN)
```

```python
import functools

import jax
import jax.numpy as jnp
import numpy as np
from jax import lax
from jax.experimental import pallas as pl
from jax.experimental.pallas import tpu as pltpu
from jax.sharding import PartitionSpec as P

NV = 6
FN = 64
CAPG = 8
CAPS = 32
TILE = 8
LANES = 128

step_size = 0.002
lift_weight = 49.0
MESH = pl.DeviceIdType.MESH
f32 = jnp.float32
bf16 = jnp.bfloat16


def cheb_matrix():
    points = -np.cos(np.pi * np.arange(8) / 7.0)
    factor = np.array([2.0, 1.0, 1.0, 1.0, 1.0, 1.0, 1.0, 2.0])
    alternating = np.where(np.arange(8) % 2 == 0, 1.0, -1.0)
    scaled = factor * alternating
    differ = points[:, None] - points[None, :] + np.eye(8)
    matrix = scaled[:, None] / scaled[None, :] / differ
    matrix = matrix * (1.0 - np.eye(8))
    return matrix - np.eye(8) * matrix.sum(axis=1)[:, None]


def plane_derivative():
    deriv_t = cheb_matrix().astype(np.float32).T
    both = np.concatenate(
        [np.kron(np.eye(16), deriv_t), np.kron(np.eye(2), np.kron(deriv_t, np.eye(8)))], axis=0
    ).astype(np.float32)
    high = both.astype(bf16)
    low = (both - high.astype(np.float32)).astype(bf16)
    return np.concatenate([high, low], axis=1)


def iota(shape, dim):
    return lax.broadcasted_iota(jnp.int32, shape, dim)


def split(x):
    high = x.astype(bf16).astype(f32)
    return high, x - high


def mm(a, b):
    return lax.dot_general(
        a.astype(bf16), b.astype(bf16), (((1,), (0,)), ((), ())), preferred_element_type=f32
    )


def mm_t(a, b):
    return lax.dot_general(
        a.astype(bf16), b.astype(bf16), (((1,), (1,)), ((), ())), preferred_element_type=f32
    )


def side(u, heat, normal):
    inverse = 1.0 / u[0]
    through = sum(n * m for n, m in zip(normal, u[1:4]) if n is not None)
    speed = through * inverse
    kinetic = 0.5 * (u[1] * u[1] + u[2] * u[2] + u[3] * u[3]) * inverse
    pressure = (heat - 1.0) * (u[4] - kinetic)
    return speed, pressure, jnp.sqrt(heat * pressure * inverse)


def flux_jump(own, other, own_heat, other_heat, normal):
    s_l, p_l, c_l = side(own, own_heat, normal)
    s_r, p_r, c_r = side(other, other_heat, normal)
    wave_l = jnp.minimum(s_l - c_l, s_r - c_r)
    wave_r = jnp.maximum(s_l + c_l, s_r + c_r)
    mass_l = own[0] * (wave_l - s_l)
    mass_r = other[0] * (wave_r - s_r)
    middle = (p_r - p_l + mass_l * s_l - mass_r * s_r) / (mass_l - mass_r)
    left = jnp.logical_or(wave_l >= 0.0, middle >= 0.0)
    u = [jnp.where(left, a, b) for a, b in zip(own, other)]
    s = jnp.where(left, s_l, s_r)
    p = jnp.where(left, p_l, p_r)
    wave = jnp.where(left, wave_l, wave_r)
    active = jnp.where(left, jnp.minimum(wave_l, 0.0), jnp.maximum(wave_r, 0.0))
    shifted = middle - s
    growth = shifted / (wave - middle)
    lifted = active * (growth + 1.0) * shifted
    scale = s + active * growth
    push = p_l - p - lifted * u[0]
    work = p_l * s_l - p * s - lifted * (u[0] * middle + p / (wave - s))
    jump = [s_l * a - scale * b for a, b in zip(own, u)]
    for d in range(3):
        if normal[d] is not None:
            jump[1 + d] = jump[1 + d] + normal[d] * push
    jump[4] = jump[4] + work
    return jump


def kernel(
    groups,
    ranks,
    material_ref,
    metric_ref,
    count_ref,
    state_ref,
    proj_ref,
    map_ref,
    nb_ref,
    deriv_ref,
    out_ref,
    send,
    recv,
    send_sem,
    recv_sem,
):
    elem = lax.axis_index("elem")
    grp = lax.axis_index("grp")
    has_up = elem + 1 < ranks
    has_down = elem > 0
    barrier = pltpu.get_barrier_semaphore()
    for off in range(1, groups):
        pl.semaphore_signal(
            barrier, inc=1, device_id=(elem, lax.rem(grp + off, groups)), device_id_type=MESH
        )

    @pl.when(has_up)
    def _():
        pl.semaphore_signal(barrier, inc=1, device_id=(elem + 1, grp), device_id_type=MESH)

    @pl.when(has_down)
    def _():
        pl.semaphore_signal(barrier, inc=1, device_id=(elem - 1, grp), device_id_type=MESH)

    slots = map_ref.shape[2]
    elems = state_ref.shape[0]
    nodes = state_ref.shape[2]
    blocks = slots // TILE
    chunks = nodes // LANES

    u = [state_ref[:, v, :] for v in range(NV)]
    heats = [1.4 + 0.27 * material_ref[j].astype(f32) for j in range(elems)]
    upper8 = iota((TILE, LANES), 1) >= FN
    col = iota((1, 256), 1)
    cell, far = col & 63, (col >> 6) & 1
    target = jnp.where(col < 128, 64 * (cell >> 3) + (cell & 7) + 56 * far, 8 * cell + 7 * far)
    pick_nodes = jnp.where(iota((nodes, 256), 0) == target, 1.0, 0.0).astype(bf16)
    high, low = split(jnp.concatenate(u, axis=0))
    both = mm(jnp.concatenate([high, low], axis=0), pick_nodes)
    flat = both[: NV * elems] + both[NV * elems :]
    trace = []
    for v in range(NV):
        rows = slice(v * elems, (v + 1) * elems)
        trace.append(
            [
                jnp.where(upper8, u[v][:, nodes - LANES :], u[v][:, :LANES]),
                flat[rows, :LANES],
                flat[rows, LANES:],
            ]
        )

    info = map_ref[0].astype(f32)
    same = iota((slots, slots), 0) == iota((slots, slots), 1)
    spread = mm(
        jnp.concatenate([jnp.where(same, info[i : i + 1], 0.0) for i in range(4)], axis=0),
        jnp.ones((slots, LANES), f32),
    ).astype(jnp.int32)
    owner, face, sub, orient = [spread[i * slots : (i + 1) * slots] for i in range(4)]
    half = jnp.where(iota((slots, LANES), 1) >= FN, 1, 0)
    upper = half == 1
    dim, end = face >> 1, face & 1

    cat = jnp.concatenate([t for ts in trace for t in ts], axis=1)
    high, low = split(cat)
    one_hot = jnp.where(owner[:, : 2 * elems] == (iota((slots, 2 * elems), 1) % elems), 1.0, 0.0)
    picked = mm(one_hot, jnp.concatenate([high, low], axis=0))
    at_end = end == half
    parts = []
    for v in range(NV):
        x, y, z = [
            picked[:, (3 * v + d) * LANES : (3 * v + d + 1) * LANES] for d in range(3)
        ]
        parts.append(jnp.where(at_end, jnp.where(dim == 0, x, jnp.where(dim == 1, y, z)), 0.0))

    col = iota((1, 512), 1)
    code, first, second = col >> 6, (col >> 3) & 7, col & 7
    swap = (code & 4) != 0
    first, second = jnp.where(swap, second, first), jnp.where(swap, first, second)
    first = jnp.where((code & 1) != 0, 7 - first, first)
    second = jnp.where((code & 2) != 0, 7 - second, second)
    turn = jnp.where((iota((LANES, 512), 0) & 63) == 8 * first + second, 1.0, 0.0).astype(bf16)
    high, low = split(jnp.concatenate(parts, axis=0))
    turned = mm(
        jnp.concatenate([high, low], axis=1), jnp.concatenate([turn, turn], axis=0)
    )
    pair = orient >> 1
    in_place = (orient & 1) == half
    parts = []
    for v in range(NV):
        a, b, c, d = [
            turned[v * slots : (v + 1) * slots, i * LANES : (i + 1) * LANES] for i in range(4)
        ]
        x = jnp.where(pair == 0, a, jnp.where(pair == 1, b, jnp.where(pair == 2, c, d)))
        parts.append(jnp.where(in_place, x, pltpu.roll(x, FN, 1)))

    quads = proj_ref[...].reshape(4 * FN, FN)
    quad_high, quad_low = split(quads)
    lhs_a, lhs_b = [], []
    for v in range(NV):
        high, low = split(parts[v])
        lhs_a.append(jnp.where(upper, low, high))
        lhs_b.append(jnp.where(upper, 0.0, high))
    projected = mm_t(
        jnp.concatenate([jnp.concatenate(lhs_a, axis=0), jnp.concatenate(lhs_b, axis=0)], axis=1),
        jnp.concatenate([quad_high, quad_high, quad_low, jnp.zeros_like(quad_low)], axis=1),
    )
    in_place = (sub & 1) != half
    native = []
    for v in range(NV):
        rows = slice(v * slots, (v + 1) * slots)
        x = jnp.where(sub >= 3, projected[rows, LANES:], projected[rows, :LANES])
        x = jnp.where(in_place, x, pltpu.roll(x, FN, 1))
        native.append(jnp.where(sub == 0, parts[v], x))
    native_heat = jnp.full((slots, LANES), heats[0], f32)
    for j in range(1, elems):
        native_heat = jnp.where(owner == j, heats[j], native_heat)

    for i in range(3):
        plane = jnp.where(upper, native[2 * i + 1], native[2 * i])
        send[:, i] = plane.reshape(blocks, TILE, LANES)
    send[:, 3] = native_heat.reshape(blocks, TILE, LANES)
    many = CAPS // TILE
    up_at, down_at = pl.ds(groups, many), pl.ds(groups + many, many)

    def to_peer(off):
        peer = lax.rem(grp + off, groups)
        return pltpu.make_async_remote_copy(
            src_ref=send.at[peer],
            dst_ref=recv.at[grp],
            send_sem=send_sem.at[off],
            recv_sem=recv_sem.at[off],
            device_id=(elem, peer),
            device_id_type=MESH,
        )

    def from_peer(off):
        peer = lax.rem(grp + groups - off, groups)
        return pltpu.make_async_remote_copy(
            src_ref=send.at[peer],
            dst_ref=recv.at[peer],
            send_sem=send_sem.at[off],
            recv_sem=recv_sem.at[off],
            device_id=(elem, peer),
            device_id_type=MESH,
        )

    def along(src, dst, sem, step):
        return pltpu.make_async_remote_copy(
            src_ref=send.at[src],
            dst_ref=recv.at[dst],
            send_sem=send_sem.at[sem],
            recv_sem=recv_sem.at[sem],
            device_id=(elem + step, grp),
            device_id_type=MESH,
        )

    up_sem, down_sem = groups, groups + 1
    pl.semaphore_wait(
        barrier, groups - 1 + has_up.astype(jnp.int32) + has_down.astype(jnp.int32)
    )

    @pl.when(has_up)
    def _():
        along(up_at, down_at, up_sem, 1).start()

    @pl.when(has_down)
    def _():
        along(down_at, up_at, down_sem, -1).start()

    for off in range(1, groups):
        to_peer(off).start()

    row8 = iota((TILE, LANES), 0)
    heat = jnp.full((TILE, LANES), heats[0], f32)
    for j in range(1, elems):
        heat = jnp.where(row8 == j, heats[j], heat)
    sign = jnp.where(upper8, 1.0, -1.0)
    across_all = nb_ref[...]
    local = []
    for d in range(3):
        across = jnp.where(
            upper8, across_all[:, 2 * d + 1 : 2 * d + 2], across_all[:, 2 * d : 2 * d + 1]
        )
        own = [trace[v][d] for v in range(NV)]
        opposite = [pltpu.roll(x, FN, 1) for x in own]
        other, other_heat = own, heat
        for j in range(elems):
            here = across == j
            other = [jnp.where(here, o[j : j + 1], x) for o, x in zip(opposite, other)]
            other_heat = jnp.where(here, heats[j], other_heat)
        normal = [None, None, None]
        normal[d] = sign
        jump = flux_jump(own, other, heat, other_heat, normal)
        local.append([jnp.where(across >= 0, x, 0.0) for x in jump])

    heat_all = jnp.concatenate([heat] * chunks, axis=1)
    inverse = 1.0 / u[0]
    velocity = [u[1 + d] * inverse for d in range(3)]
    kinetic = 0.5 * (u[1] * velocity[0] + u[2] * velocity[1] + u[3] * velocity[2])
    pressure = (heat_all - 1.0) * (u[4] - kinetic)

    def flux(d):
        s = velocity[d]
        f = [u[1 + d]] + [m * s for m in u[1:4]] + [(u[4] + pressure) * s, u[5] * s]
        f[1 + d] = f[1 + d] + pressure
        return f

    def cut(x):
        return [x[:, i * LANES : (i + 1) * LANES] for i in range(chunks)]

    deriv = cheb_matrix()
    flux_x, flux_y, flux_z = [[cut(f) for f in flux(d)] for d in range(3)]
    stacked = jnp.concatenate(
        [
            jnp.concatenate([flux_z[v][i], flux_y[v][i]], axis=1)
            for v in range(NV)
            for i in range(chunks)
        ],
        axis=0,
    )
    high, low = split(stacked)
    rows = NV * chunks * TILE
    both = mm(jnp.concatenate([high, low], axis=0), deriv_ref[...])
    plane_sum = both[:rows, :LANES] + both[:rows, LANES:] + both[rows:, :LANES]
    rolled_x = [[pltpu.roll(x, FN, 1) for x in flux_x[v]] for v in range(NV)]
    volume = [[None] * chunks for _ in range(NV)]
    for j in range(chunks):
        weights = []
        for i in range(chunks):
            straight = jnp.where(
                upper8, float(deriv[2 * j + 1, 2 * i + 1]), float(deriv[2 * j, 2 * i])
            )
            crossed = jnp.where(
                upper8, float(deriv[2 * j + 1, 2 * i]), float(deriv[2 * j, 2 * i + 1])
            )
            weights.append((straight, crossed))
        for v in range(NV):
            at = (v * chunks + j) * TILE
            total = plane_sum[at : at + TILE]
            for i in range(chunks):
                total = total + weights[i][0] * flux_x[v][i] + weights[i][1] * rolled_x[v][i]
            volume[v][j] = -total

    row = iota((TILE, LANES), 0)
    live = [row < count_ref[0, g] for g in range(groups)]
    for side_at in (groups, groups + 1):
        live += [row + TILE * i < count_ref[0, side_at] for i in range(many)]
    live = jnp.concatenate([jnp.where(x, 1.0, 0.0) for x in live], axis=0) > 0.0
    sign = jnp.where(end == 1, 1.0, -1.0)
    normal = [jnp.where(dim == d, sign, 0.0) for d in range(3)]
    back_weight = jnp.where(sub == 0, 1.0, 0.25)

    for off in range(1, groups):
        from_peer(off).wait_recv()

    @pl.when(has_up)
    def _():
        along(down_at, up_at, down_sem, 1).wait_recv()

    @pl.when(has_down)
    def _():
        along(up_at, down_at, up_sem, -1).wait_recv()

    partner = []
    for i in range(3):
        plane = recv[:, i].reshape(slots, LANES)
        moved = pltpu.roll(plane, FN, 1)
        partner += [jnp.where(upper, moved, plane), jnp.where(upper, plane, moved)]
    partner = [jnp.where(live, a, b) for a, b in zip(partner, native)]
    partner_heat = jnp.where(live, recv[:, 3].reshape(slots, LANES), native_heat)
    jump = flux_jump(native, partner, native_heat, partner_heat, normal)
    corr = [jnp.where(live, back_weight * x, 0.0) for x in jump]

    in_a, in_b = sub == 1 + half, sub == 3 + half
    highs, lows = [], []
    for v in range(NV):
        high, low = split(corr[v])
        for kept, x in ((highs, high), (lows, low)):
            kept.append(
                jnp.concatenate([jnp.where(in_a, x, 0.0), jnp.where(in_b, x, 0.0)], axis=1)
            )
    both = mm(
        jnp.concatenate(highs + lows, axis=0),
        jnp.concatenate([quad_high, quad_high, quad_low, quad_low], axis=1),
    )
    lhs_high, lhs_low = [], []
    for v in range(NV):
        h = both[v * slots : (v + 1) * slots]
        l = both[(NV + v) * slots : (NV + v + 1) * slots]
        x = jnp.where(sub == 0, corr[v], h[:, :LANES] + h[:, LANES:] + l[:, :LANES])
        high, low = split(x)
        for kept, y in ((lhs_high, high), (lhs_low, low)):
            kept.append(
                jnp.concatenate(
                    [jnp.where(orient == 2 * i + half, y, 0.0) for i in range(4)], axis=1
                )
            )
    both = mm_t(jnp.concatenate(lhs_high + lhs_low, axis=0), turn)
    placed = []
    for v in range(NV):
        x = both[v * slots : (v + 1) * slots] + both[(NV + v) * slots : (NV + v + 1) * slots]
        x = jnp.where(at_end, x, 0.0)
        placed += [jnp.where(dim == d, x, 0.0) for d in range(3)]
    high, low = split(jnp.concatenate(placed, axis=1))
    gather = jnp.where(iota((elems, slots), 0) == map_ref[0, 0:1, :], 1.0, 0.0)
    face_sum = mm(gather, high) + mm(gather, low)

    lines = []
    for v in range(NV):
        at = 3 * v * LANES
        lines.append([face_sum[:, at + d * LANES : at + (d + 1) * LANES] + local[d][v] for d in range(3)])
    wide = jnp.concatenate([jnp.concatenate(x[1:], axis=1) for x in lines], axis=0)
    high, low = split(wide)
    both = mm_t(jnp.concatenate([high, low], axis=0), pick_nodes)
    surface = both[: NV * elems] + both[NV * elems :]
    scale = jnp.full((TILE, LANES), metric_ref[0], f32)
    for j in range(1, elems):
        scale = jnp.where(row8 == j, metric_ref[j], scale)
    scale = step_size * scale
    for v in range(NV):
        for j in range(chunks):
            s = surface[v * elems : (v + 1) * elems, j * LANES : (j + 1) * LANES]
            if j == 0:
                s = s + jnp.where(upper8, 0.0, lines[v][0])
            if j == chunks - 1:
                s = s + jnp.where(upper8, lines[v][0], 0.0)
            at = slice(j * LANES, (j + 1) * LANES)
            out_ref[:, v, at] = u[v][:, at] + scale * (volume[v][j] + lift_weight * s)

    for off in range(1, groups):
        to_peer(off).wait_send()

    @pl.when(has_up)
    def _():
        along(up_at, down_at, up_sem, 1).wait_send()

    @pl.when(has_down)
    def _():
        along(down_at, up_at, down_sem, -1).wait_send()


def shards(state, material, metric, mortar_proj, mortar_map, mortar_count, neighbours):
    groups, ranks = lax.axis_size("grp"), lax.axis_size("elem")
    blocks = mortar_map.shape[2] // TILE
    vmem = pl.BlockSpec(memory_space=pltpu.VMEM)
    smem = pl.BlockSpec(memory_space=pltpu.SMEM)
    return pl.pallas_call(
        functools.partial(kernel, groups, ranks),
        out_shape=jax.ShapeDtypeStruct(state.shape, state.dtype),
        in_specs=[smem] * 3 + [vmem] * 5,
        out_specs=vmem,
        scratch_shapes=[
            pltpu.VMEM((blocks, 4, TILE, LANES), f32),
            pltpu.VMEM((blocks, 4, TILE, LANES), f32),
            pltpu.SemaphoreType.DMA((groups + 2,)),
            pltpu.SemaphoreType.DMA((groups + 2,)),
        ],
        compiler_params=pltpu.CompilerParams(
            collective_id=0, has_side_effects=True, vmem_limit_bytes=40 * 2**20
        ),
    )(
        material,
        metric,
        mortar_count,
        state,
        mortar_proj,
        mortar_map,
        neighbours,
        jnp.asarray(plane_derivative()),
    )


def solution(mesh):
    return jax.shard_map(
        shards,
        mesh=mesh,
        in_specs=(
            P(("elem", "grp"), None, None),
            P(("elem", "grp")),
            P(("elem", "grp")),
            P(),
            P(("elem", "grp"), None, None),
            P(("elem", "grp"), None),
            P(("elem", "grp"), None),
        ),
        out_specs=P(("elem", "grp"), None, None),
        check_vma=False,
    )
```

```python
import functools

import jax
import jax.numpy as jnp
import numpy as np
from jax import lax
from jax.experimental import pallas as pl
from jax.experimental.pallas import tpu as pltpu
from jax.sharding import PartitionSpec as P

NV = 6
FN = 64
CAPG = 8
CAPS = 32
TILE = 8
LANES = 128

step_size = 0.002
lift_weight = 49.0
MESH = pl.DeviceIdType.MESH
f32 = jnp.float32
bf16 = jnp.bfloat16


def cheb_matrix():
    points = -np.cos(np.pi * np.arange(8) / 7.0)
    factor = np.array([2.0, 1.0, 1.0, 1.0, 1.0, 1.0, 1.0, 2.0])
    alternating = np.where(np.arange(8) % 2 == 0, 1.0, -1.0)
    scaled = factor * alternating
    differ = points[:, None] - points[None, :] + np.eye(8)
    matrix = scaled[:, None] / scaled[None, :] / differ
    matrix = matrix * (1.0 - np.eye(8))
    return matrix - np.eye(8) * matrix.sum(axis=1)[:, None]


def plane_derivative():
    deriv_t = cheb_matrix().astype(np.float32).T
    both = np.concatenate(
        [np.kron(np.eye(16), deriv_t), np.kron(np.eye(2), np.kron(deriv_t, np.eye(8)))], axis=0
    ).astype(np.float32)
    high = both.astype(bf16)
    low = (both - high.astype(np.float32)).astype(bf16)
    return np.concatenate([high, low], axis=1)


def iota(shape, dim):
    return lax.broadcasted_iota(jnp.int32, shape, dim)


def split(x):
    high = x.astype(bf16).astype(f32)
    return high, x - high


def mm(a, b):
    return lax.dot_general(
        a.astype(bf16), b.astype(bf16), (((1,), (0,)), ((), ())), preferred_element_type=f32
    )


def mm_t(a, b):
    return lax.dot_general(
        a.astype(bf16), b.astype(bf16), (((1,), (1,)), ((), ())), preferred_element_type=f32
    )


def side(u, heat, normal):
    inverse = 1.0 / u[0]
    through = sum(n * m for n, m in zip(normal, u[1:4]) if n is not None)
    speed = through * inverse
    kinetic = 0.5 * (u[1] * u[1] + u[2] * u[2] + u[3] * u[3]) * inverse
    pressure = (heat - 1.0) * (u[4] - kinetic)
    return speed, pressure, jnp.sqrt(heat * pressure * inverse)


def flux_jump(own, other, own_heat, other_heat, normal):
    s_l, p_l, c_l = side(own, own_heat, normal)
    s_r, p_r, c_r = side(other, other_heat, normal)
    wave_l = jnp.minimum(s_l - c_l, s_r - c_r)
    wave_r = jnp.maximum(s_l + c_l, s_r + c_r)
    mass_l = own[0] * (wave_l - s_l)
    mass_r = other[0] * (wave_r - s_r)
    middle = (p_r - p_l + mass_l * s_l - mass_r * s_r) / (mass_l - mass_r)
    left = jnp.logical_or(wave_l >= 0.0, middle >= 0.0)
    u = [jnp.where(left, a, b) for a, b in zip(own, other)]
    s = jnp.where(left, s_l, s_r)
    p = jnp.where(left, p_l, p_r)
    wave = jnp.where(left, wave_l, wave_r)
    active = jnp.where(left, jnp.minimum(wave_l, 0.0), jnp.maximum(wave_r, 0.0))
    shifted = middle - s
    growth = shifted / (wave - middle)
    lifted = active * (growth + 1.0) * shifted
    scale = s + active * growth
    push = p_l - p - lifted * u[0]
    work = p_l * s_l - p * s - lifted * (u[0] * middle + p / (wave - s))
    jump = [s_l * a - scale * b for a, b in zip(own, u)]
    for d in range(3):
        if normal[d] is not None:
            jump[1 + d] = jump[1 + d] + normal[d] * push
    jump[4] = jump[4] + work
    return jump


def chosen_turn(turned, orient, half):
    slots = orient.shape[0]
    pair = orient >> 1
    in_place = (orient & 1) == half
    result = []
    for v in range(NV):
        a, b, c, d = [
            turned[v * slots : (v + 1) * slots, i * LANES : (i + 1) * LANES] for i in range(4)
        ]
        x = jnp.where(pair == 0, a, jnp.where(pair == 1, b, jnp.where(pair == 2, c, d)))
        result.append(jnp.where(in_place, x, pltpu.roll(x, FN, 1)))
    return result


def split_columns(parts, upper):
    first, second = [], []
    for x in parts:
        high, low = split(x)
        first.append(jnp.where(upper, low, high))
        second.append(jnp.where(upper, 0.0, high))
    return jnp.concatenate(
        [jnp.concatenate(first, axis=0), jnp.concatenate(second, axis=0)], axis=1
    )


def chosen_quad(projected, parts, sub, half):
    slots = sub.shape[0]
    in_place = (sub & 1) != half
    result = []
    for v in range(NV):
        rows = slice(v * slots, (v + 1) * slots)
        x = jnp.where(sub >= 3, projected[rows, LANES:], projected[rows, :LANES])
        x = jnp.where(in_place, x, pltpu.roll(x, FN, 1))
        result.append(jnp.where(sub == 0, parts[v], x))
    return result


def kernel(
    groups,
    ranks,
    state_hbm,
    map_hbm,
    material_hbm,
    proj_hbm,
    nb_hbm,
    count_hbm,
    metric_hbm,
    deriv_hbm,
    out_ref,
    state_ref,
    map_ref,
    material_ref,
    proj_ref,
    nb_ref,
    count_ref,
    metric_ref,
    deriv_ref,
    send,
    recv,
    send_sem,
    recv_sem,
    fetch_sem,
):
    fetches = [
        pltpu.make_async_copy(src, dst, fetch_sem.at[i])
        for i, (src, dst) in enumerate(
            (
                (state_hbm, state_ref),
                (map_hbm, map_ref),
                (material_hbm, material_ref),
                (proj_hbm, proj_ref),
                (nb_hbm, nb_ref),
                (count_hbm, count_ref),
                (metric_hbm, metric_ref),
                (deriv_hbm, deriv_ref),
            )
        )
    ]
    for fetch in fetches:
        fetch.start()
    elem = lax.axis_index("elem")
    grp = lax.axis_index("grp")
    has_up = elem + 1 < ranks
    has_down = elem > 0
    barrier = pltpu.get_barrier_semaphore()
    for off in range(1, groups):
        pl.semaphore_signal(
            barrier, inc=1, device_id=(elem, lax.rem(grp + off, groups)), device_id_type=MESH
        )

    @pl.when(has_up)
    def _():
        pl.semaphore_signal(barrier, inc=1, device_id=(elem + 1, grp), device_id_type=MESH)

    @pl.when(has_down)
    def _():
        pl.semaphore_signal(barrier, inc=1, device_id=(elem - 1, grp), device_id_type=MESH)

    slots = map_ref.shape[2]
    elems = state_ref.shape[1]
    nodes = state_ref.shape[2]
    blocks = slots // TILE
    chunks = nodes // LANES

    upper8 = iota((TILE, LANES), 1) >= FN
    col = iota((1, 256), 1)
    cell, far = col & 63, (col >> 6) & 1
    target = jnp.where(col < 128, 64 * (cell >> 3) + (cell & 7) + 56 * far, 8 * cell + 7 * far)
    pick_nodes = jnp.where(iota((nodes, 256), 0) == target, 1.0, 0.0).astype(bf16)
    col = iota((1, 512), 1)
    code, first, second = col >> 6, (col >> 3) & 7, col & 7
    swap = (code & 4) != 0
    first, second = jnp.where(swap, second, first), jnp.where(swap, first, second)
    first = jnp.where((code & 1) != 0, 7 - first, first)
    second = jnp.where((code & 2) != 0, 7 - second, second)
    turn = jnp.where((iota((LANES, 512), 0) & 63) == 8 * first + second, 1.0, 0.0).astype(bf16)
    same = iota((slots, slots), 0) == iota((slots, slots), 1)
    for fetch in fetches[:3]:
        fetch.wait()
    u = [state_ref[v] for v in range(NV)]
    heats = [1.4 + 0.27 * material_ref[j].astype(f32) for j in range(elems)]
    high, low = split(jnp.concatenate(u, axis=0))
    both = mm(jnp.concatenate([high, low], axis=0), pick_nodes)
    flat = both[: NV * elems] + both[NV * elems :]
    trace = []
    for v in range(NV):
        rows = slice(v * elems, (v + 1) * elems)
        trace.append(
            [
                jnp.where(upper8, u[v][:, nodes - LANES :], u[v][:, :LANES]),
                flat[rows, :LANES],
                flat[rows, LANES:],
            ]
        )

    info = map_ref[0].astype(f32)
    spread = mm(
        jnp.concatenate([jnp.where(same, info[i : i + 1], 0.0) for i in range(4)], axis=0),
        jnp.ones((slots, LANES), f32),
    ).astype(jnp.int32)
    owner, face, sub, orient = [spread[i * slots : (i + 1) * slots] for i in range(4)]
    half = jnp.where(iota((slots, LANES), 1) >= FN, 1, 0)
    upper = half == 1
    dim, end = face >> 1, face & 1

    high, low = split(
        jnp.concatenate(
            [jnp.concatenate([trace[v][d] for v in range(NV)], axis=1) for d in range(3)], axis=0
        )
    )
    rows = 3 * elems
    place = dim * elems + owner
    one_hot = jnp.where(place[:, : 2 * rows] == (iota((slots, 2 * rows), 1) % rows), 1.0, 0.0)
    picked = mm(one_hot, jnp.concatenate([high, low], axis=0))
    at_end = end == half
    parts = [
        jnp.where(at_end, picked[:, v * LANES : (v + 1) * LANES], 0.0) for v in range(NV)
    ]

    high, low = split(jnp.concatenate(parts, axis=0))
    turned = mm(
        jnp.concatenate([high, low], axis=1), jnp.concatenate([turn, turn], axis=0)
    )
    parts = chosen_turn(turned, orient, half)

    fetches[3].wait()
    quads = proj_ref[...].reshape(4 * FN, FN)
    quad_high, quad_low = split(quads)
    projected = mm_t(
        split_columns(parts, upper),
        jnp.concatenate([quad_high, quad_high, quad_low, jnp.zeros_like(quad_low)], axis=1),
    )
    native = chosen_quad(projected, parts, sub, half)
    native_heat = jnp.full((slots, LANES), heats[0], f32)
    for j in range(1, elems):
        native_heat = jnp.where(owner == j, heats[j], native_heat)

    for i in range(3):
        plane = jnp.where(upper, native[2 * i + 1], native[2 * i])
        send[:, i] = plane.reshape(blocks, TILE, LANES)
    send[:, 3] = native_heat.reshape(blocks, TILE, LANES)
    many = CAPS // TILE
    up_at, down_at = pl.ds(groups, many), pl.ds(groups + many, many)

    def to_peer(off):
        peer = lax.rem(grp + off, groups)
        return pltpu.make_async_remote_copy(
            src_ref=send.at[peer],
            dst_ref=recv.at[grp],
            send_sem=send_sem.at[off],
            recv_sem=recv_sem.at[off],
            device_id=(elem, peer),
            device_id_type=MESH,
        )

    def from_peer(off):
        peer = lax.rem(grp + groups - off, groups)
        return pltpu.make_async_remote_copy(
            src_ref=send.at[peer],
            dst_ref=recv.at[peer],
            send_sem=send_sem.at[off],
            recv_sem=recv_sem.at[off],
            device_id=(elem, peer),
            device_id_type=MESH,
        )

    def along(src, dst, sem, step):
        return pltpu.make_async_remote_copy(
            src_ref=send.at[src],
            dst_ref=recv.at[dst],
            send_sem=send_sem.at[sem],
            recv_sem=recv_sem.at[sem],
            device_id=(elem + step, grp),
            device_id_type=MESH,
        )

    up_sem, down_sem = groups, groups + 1
    pl.semaphore_wait(
        barrier, groups - 1 + has_up.astype(jnp.int32) + has_down.astype(jnp.int32)
    )

    @pl.when(has_up)
    def _():
        along(up_at, down_at, up_sem, 1).start()

    @pl.when(has_down)
    def _():
        along(down_at, up_at, down_sem, -1).start()

    for off in range(1, groups):
        to_peer(off).start()

    for fetch in fetches[4:]:
        fetch.wait()
    row8 = iota((TILE, LANES), 0)
    heat = jnp.full((TILE, LANES), heats[0], f32)
    for j in range(1, elems):
        heat = jnp.where(row8 == j, heats[j], heat)
    sign = jnp.where(upper8, 1.0, -1.0)
    across_all = nb_ref[...]
    local = []
    for d in range(3):
        across = jnp.where(
            upper8, across_all[:, 2 * d + 1 : 2 * d + 2], across_all[:, 2 * d : 2 * d + 1]
        )
        own = [trace[v][d] for v in range(NV)]
        opposite = [pltpu.roll(x, FN, 1) for x in own]
        other, other_heat = own, heat
        for j in range(elems):
            here = across == j
            other = [jnp.where(here, o[j : j + 1], x) for o, x in zip(opposite, other)]
            other_heat = jnp.where(here, heats[j], other_heat)
        normal = [None, None, None]
        normal[d] = sign
        jump = flux_jump(own, other, heat, other_heat, normal)
        local.append([jnp.where(across >= 0, x, 0.0) for x in jump])

    heat_all = jnp.concatenate([heat] * chunks, axis=1)
    inverse = 1.0 / u[0]
    velocity = [u[1 + d] * inverse for d in range(3)]
    kinetic = 0.5 * (u[1] * velocity[0] + u[2] * velocity[1] + u[3] * velocity[2])
    pressure = (heat_all - 1.0) * (u[4] - kinetic)

    def flux(d):
        s = velocity[d]
        f = [u[1 + d]] + [m * s for m in u[1:4]] + [(u[4] + pressure) * s, u[5] * s]
        f[1 + d] = f[1 + d] + pressure
        return f

    def cut(x):
        return [x[:, i * LANES : (i + 1) * LANES] for i in range(chunks)]

    deriv = cheb_matrix()
    flux_x, flux_y, flux_z = [[cut(f) for f in flux(d)] for d in range(3)]
    stacked = jnp.concatenate(
        [
            jnp.concatenate([flux_z[v][i], flux_y[v][i]], axis=1)
            for v in range(NV)
            for i in range(chunks)
        ],
        axis=0,
    )
    high, low = split(stacked)
    rows = NV * chunks * TILE
    both = mm(jnp.concatenate([high, low], axis=0), deriv_ref[...])
    plane_sum = both[:rows, :LANES] + both[:rows, LANES:] + both[rows:, :LANES]
    rolled_x = [[pltpu.roll(x, FN, 1) for x in flux_x[v]] for v in range(NV)]
    volume = [[None] * chunks for _ in range(NV)]
    for j in range(chunks):
        weights = []
        for i in range(chunks):
            straight = jnp.where(
                upper8, float(deriv[2 * j + 1, 2 * i + 1]), float(deriv[2 * j, 2 * i])
            )
            crossed = jnp.where(
                upper8, float(deriv[2 * j + 1, 2 * i]), float(deriv[2 * j, 2 * i + 1])
            )
            weights.append((straight, crossed))
        for v in range(NV):
            at = (v * chunks + j) * TILE
            total = plane_sum[at : at + TILE]
            for i in range(chunks):
                total = total + weights[i][0] * flux_x[v][i] + weights[i][1] * rolled_x[v][i]
            volume[v][j] = -total

    row = iota((TILE, LANES), 0)
    live = [row < count_ref[0, g] for g in range(groups)]
    for side_at in (groups, groups + 1):
        live += [row + TILE * i < count_ref[0, side_at] for i in range(many)]
    live = jnp.concatenate([jnp.where(x, 1.0, 0.0) for x in live], axis=0) > 0.0
    sign = jnp.where(end == 1, 1.0, -1.0)
    normal = [jnp.where(dim == d, sign, 0.0) for d in range(3)]
    back_weight = jnp.where(sub == 0, 1.0, 0.25)
    across_quads = jnp.concatenate([proj_ref[i] for i in range(4)], axis=1)
    quad_high, quad_low = split(across_quads)
    quads_back = jnp.concatenate(
        [quad_high, quad_high, quad_low, jnp.zeros_like(quad_low)], axis=0
    ).astype(bf16)
    back_orient = jnp.where(orient >= 5, jnp.where(orient == 7, 7, 11 - orient), orient)
    gather_at = (map_ref[0, 1:2, :] >> 1) * elems + map_ref[0, 0:1, :]
    gather = jnp.where(iota((3 * elems, slots), 0) == gather_at, 1.0, 0.0).astype(bf16)

    for off in range(1, groups):
        from_peer(off).wait_recv()

    @pl.when(has_up)
    def _():
        along(down_at, up_at, down_sem, 1).wait_recv()

    @pl.when(has_down)
    def _():
        along(up_at, down_at, up_sem, -1).wait_recv()

    partner = []
    for i in range(3):
        plane = recv[:, i].reshape(slots, LANES)
        moved = pltpu.roll(plane, FN, 1)
        partner += [jnp.where(upper, moved, plane), jnp.where(upper, plane, moved)]
    partner = [jnp.where(live, a, b) for a, b in zip(partner, native)]
    partner_heat = jnp.where(live, recv[:, 3].reshape(slots, LANES), native_heat)
    jump = flux_jump(native, partner, native_heat, partner_heat, normal)
    corr = [jnp.where(live, back_weight * x, 0.0) for x in jump]

    parts = chosen_quad(mm(split_columns(corr, upper), quads_back), corr, sub, half)
    lhs = []
    for x in parts:
        high, low = split(x)
        lhs.append(jnp.where(upper, low, high))
    parts = chosen_turn(mm(jnp.concatenate(lhs, axis=0), turn), back_orient, half)
    high, low = split(
        jnp.concatenate([jnp.where(at_end, x, 0.0) for x in parts], axis=1)
    )
    face_sum = mm(gather, high) + mm(gather, low)

    lines = []
    for v in range(NV):
        at = slice(v * LANES, (v + 1) * LANES)
        lines.append(
            [face_sum[d * elems : (d + 1) * elems, at] + local[d][v] for d in range(3)]
        )
    wide = jnp.concatenate([jnp.concatenate(x[1:], axis=1) for x in lines], axis=0)
    high, low = split(wide)
    both = mm_t(jnp.concatenate([high, low], axis=0), pick_nodes)
    surface = both[: NV * elems] + both[NV * elems :]
    scale = jnp.full((TILE, LANES), metric_ref[0], f32)
    for j in range(1, elems):
        scale = jnp.where(row8 == j, metric_ref[j], scale)
    scale = step_size * scale
    for v in range(NV):
        for j in range(chunks):
            s = surface[v * elems : (v + 1) * elems, j * LANES : (j + 1) * LANES]
            if j == 0:
                s = s + jnp.where(upper8, 0.0, lines[v][0])
            if j == chunks - 1:
                s = s + jnp.where(upper8, lines[v][0], 0.0)
            at = slice(j * LANES, (j + 1) * LANES)
            out_ref[v, :, at] = u[v][:, at] + scale * (volume[v][j] + lift_weight * s)

    for off in range(1, groups):
        to_peer(off).wait_send()

    @pl.when(has_up)
    def _():
        along(up_at, down_at, up_sem, 1).wait_send()

    @pl.when(has_down)
    def _():
        along(down_at, up_at, down_sem, -1).wait_send()


def shards(state, material, metric, mortar_proj, mortar_map, mortar_count, neighbours):
    groups, ranks = lax.axis_size("grp"), lax.axis_size("elem")
    blocks = mortar_map.shape[2] // TILE
    by_variable = jnp.transpose(state, (1, 0, 2))
    operands = (
        by_variable,
        mortar_map,
        material,
        mortar_proj,
        neighbours,
        mortar_count,
        metric,
        jnp.asarray(plane_derivative()),
    )
    in_smem = (2, 5, 6)
    result = pl.pallas_call(
        functools.partial(kernel, groups, ranks),
        out_shape=jax.ShapeDtypeStruct(by_variable.shape, state.dtype),
        in_specs=[pl.BlockSpec(memory_space=pltpu.HBM)] * len(operands),
        out_specs=pl.BlockSpec(memory_space=pltpu.VMEM),
        scratch_shapes=[
            (pltpu.SMEM if i in in_smem else pltpu.VMEM)(x.shape, x.dtype)
            for i, x in enumerate(operands)
        ]
        + [
            pltpu.VMEM((blocks, 4, TILE, LANES), f32),
            pltpu.VMEM((blocks, 4, TILE, LANES), f32),
            pltpu.SemaphoreType.DMA((groups + 2,)),
            pltpu.SemaphoreType.DMA((groups + 2,)),
            pltpu.SemaphoreType.DMA((len(operands),)),
        ],
        compiler_params=pltpu.CompilerParams(
            collective_id=0, has_side_effects=True, vmem_limit_bytes=56 * 2**20
        ),
    )(*operands)
    return jnp.transpose(result, (1, 0, 2))


def solution(mesh):
    return jax.shard_map(
        shards,
        mesh=mesh,
        in_specs=(
            P(("elem", "grp"), None, None),
            P(("elem", "grp")),
            P(("elem", "grp")),
            P(),
            P(("elem", "grp"), None, None),
            P(("elem", "grp"), None),
            P(("elem", "grp"), None),
        ),
        out_specs=P(("elem", "grp"), None, None),
        check_vma=False,
    )
```

```python
import functools

import jax
import jax.numpy as jnp
import numpy as np
from jax import lax
from jax.experimental import pallas as pl
from jax.experimental.pallas import tpu as pltpu
from jax.sharding import PartitionSpec as P

NV = 6
FN = 64
CAPG = 8
CAPS = 32
TILE = 8
LANES = 128

step_size = 0.002
lift_weight = 49.0
MESH = pl.DeviceIdType.MESH
f32 = jnp.float32
bf16 = jnp.bfloat16


def cheb_matrix():
    points = -np.cos(np.pi * np.arange(8) / 7.0)
    factor = np.array([2.0, 1.0, 1.0, 1.0, 1.0, 1.0, 1.0, 2.0])
    alternating = np.where(np.arange(8) % 2 == 0, 1.0, -1.0)
    scaled = factor * alternating
    differ = points[:, None] - points[None, :] + np.eye(8)
    matrix = scaled[:, None] / scaled[None, :] / differ
    matrix = matrix * (1.0 - np.eye(8))
    return matrix - np.eye(8) * matrix.sum(axis=1)[:, None]


def plane_derivative():
    deriv_t = cheb_matrix().astype(np.float32).T
    both = np.concatenate(
        [np.kron(np.eye(16), deriv_t), np.kron(np.eye(2), np.kron(deriv_t, np.eye(8)))], axis=0
    ).astype(np.float32)
    high = both.astype(bf16)
    low = (both - high.astype(np.float32)).astype(bf16)
    return np.concatenate([high, low], axis=1)


def iota(shape, dim):
    return lax.broadcasted_iota(jnp.int32, shape, dim)


def split(x):
    high = x.astype(bf16).astype(f32)
    return high, x - high


def mm(a, b):
    return lax.dot_general(
        a.astype(bf16), b.astype(bf16), (((1,), (0,)), ((), ())), preferred_element_type=f32
    )


def mm_t(a, b):
    return lax.dot_general(
        a.astype(bf16), b.astype(bf16), (((1,), (1,)), ((), ())), preferred_element_type=f32
    )


def side(u, heat, normal):
    inverse = 1.0 / u[0]
    through = sum(n * m for n, m in zip(normal, u[1:4]) if n is not None)
    speed = through * inverse
    kinetic = 0.5 * (u[1] * u[1] + u[2] * u[2] + u[3] * u[3]) * inverse
    pressure = (heat - 1.0) * (u[4] - kinetic)
    return speed, pressure, jnp.sqrt(heat * pressure * inverse)


def flux_jump(own, other, own_heat, other_heat, normal):
    s_l, p_l, c_l = side(own, own_heat, normal)
    s_r, p_r, c_r = side(other, other_heat, normal)
    wave_l = jnp.minimum(s_l - c_l, s_r - c_r)
    wave_r = jnp.maximum(s_l + c_l, s_r + c_r)
    mass_l = own[0] * (wave_l - s_l)
    mass_r = other[0] * (wave_r - s_r)
    middle = (p_r - p_l + mass_l * s_l - mass_r * s_r) / (mass_l - mass_r)
    left = jnp.logical_or(wave_l >= 0.0, middle >= 0.0)
    u = [jnp.where(left, a, b) for a, b in zip(own, other)]
    s = jnp.where(left, s_l, s_r)
    p = jnp.where(left, p_l, p_r)
    wave = jnp.where(left, wave_l, wave_r)
    active = jnp.where(left, jnp.minimum(wave_l, 0.0), jnp.maximum(wave_r, 0.0))
    shifted = middle - s
    growth = shifted / (wave - middle)
    lifted = active * (growth + 1.0) * shifted
    scale = s + active * growth
    push = p_l - p - lifted * u[0]
    work = p_l * s_l - p * s - lifted * (u[0] * middle + p / (wave - s))
    jump = [s_l * a - scale * b for a, b in zip(own, u)]
    for d in range(3):
        if normal[d] is not None:
            jump[1 + d] = jump[1 + d] + normal[d] * push
    jump[4] = jump[4] + work
    return jump


def chosen_turn(turned, orient, half):
    slots = orient.shape[0]
    pair = orient >> 1
    in_place = (orient & 1) == half
    result = []
    for v in range(NV):
        a, b, c, d = [
            turned[v * slots : (v + 1) * slots, i * LANES : (i + 1) * LANES] for i in range(4)
        ]
        x = jnp.where(pair == 0, a, jnp.where(pair == 1, b, jnp.where(pair == 2, c, d)))
        result.append(jnp.where(in_place, x, pltpu.roll(x, FN, 1)))
    return result


def split_columns(parts, upper):
    first, second = [], []
    for x in parts:
        high, low = split(x)
        first.append(jnp.where(upper, low, high))
        second.append(jnp.where(upper, 0.0, high))
    return jnp.concatenate(
        [jnp.concatenate(first, axis=0), jnp.concatenate(second, axis=0)], axis=1
    )


def chosen_quad(projected, parts, sub, half):
    slots = sub.shape[0]
    in_place = (sub & 1) != half
    result = []
    for v in range(NV):
        rows = slice(v * slots, (v + 1) * slots)
        x = jnp.where(sub >= 3, projected[rows, LANES:], projected[rows, :LANES])
        x = jnp.where(in_place, x, pltpu.roll(x, FN, 1))
        result.append(jnp.where(sub == 0, parts[v], x))
    return result


def kernel(
    groups,
    ranks,
    state_hbm,
    map_hbm,
    material_hbm,
    proj_hbm,
    nb_hbm,
    count_hbm,
    metric_hbm,
    deriv_hbm,
    out_ref,
    state_ref,
    map_ref,
    material_ref,
    proj_ref,
    nb_ref,
    count_ref,
    metric_ref,
    deriv_ref,
    send,
    recv,
    send_sem,
    recv_sem,
    fetch_sem,
):
    fetches = [
        pltpu.make_async_copy(src, dst, fetch_sem.at[i])
        for i, (src, dst) in enumerate(
            (
                (state_hbm, state_ref),
                (map_hbm, map_ref),
                (material_hbm, material_ref),
                (proj_hbm, proj_ref),
                (nb_hbm, nb_ref),
                (count_hbm, count_ref),
                (metric_hbm, metric_ref),
                (deriv_hbm, deriv_ref),
            )
        )
    ]
    for fetch in fetches:
        fetch.start()
    elem = lax.axis_index("elem")
    grp = lax.axis_index("grp")
    has_up = elem + 1 < ranks
    has_down = elem > 0
    barrier = pltpu.get_barrier_semaphore()
    for off in range(1, groups):
        pl.semaphore_signal(
            barrier, inc=1, device_id=(elem, lax.rem(grp + off, groups)), device_id_type=MESH
        )

    @pl.when(has_up)
    def _():
        pl.semaphore_signal(barrier, inc=1, device_id=(elem + 1, grp), device_id_type=MESH)

    @pl.when(has_down)
    def _():
        pl.semaphore_signal(barrier, inc=1, device_id=(elem - 1, grp), device_id_type=MESH)

    slots = map_ref.shape[2]
    elems = state_ref.shape[1]
    nodes = state_ref.shape[2]
    blocks = slots // TILE
    chunks = nodes // LANES

    upper8 = iota((TILE, LANES), 1) >= FN
    col = iota((1, 256), 1)
    cell, far = col & 63, (col >> 6) & 1
    target = jnp.where(col < 128, 64 * (cell >> 3) + (cell & 7) + 56 * far, 8 * cell + 7 * far)
    pick_nodes = jnp.where(iota((nodes, 256), 0) == target, 1.0, 0.0).astype(bf16)
    col = iota((1, 512), 1)
    code, first, second = col >> 6, (col >> 3) & 7, col & 7
    swap = (code & 4) != 0
    first, second = jnp.where(swap, second, first), jnp.where(swap, first, second)
    first = jnp.where((code & 1) != 0, 7 - first, first)
    second = jnp.where((code & 2) != 0, 7 - second, second)
    turn = jnp.where((iota((LANES, 512), 0) & 63) == 8 * first + second, 1.0, 0.0).astype(bf16)
    same = iota((slots, slots), 0) == iota((slots, slots), 1)
    for fetch in fetches[:3]:
        fetch.wait()
    u = [state_ref[v] for v in range(NV)]
    heats = [1.4 + 0.27 * material_ref[j].astype(f32) for j in range(elems)]
    high, low = split(jnp.concatenate(u, axis=0))
    both = mm(jnp.concatenate([high, low], axis=0), pick_nodes)
    flat = both[: NV * elems] + both[NV * elems :]
    trace = []
    for v in range(NV):
        rows = slice(v * elems, (v + 1) * elems)
        trace.append(
            [
                jnp.where(upper8, u[v][:, nodes - LANES :], u[v][:, :LANES]),
                flat[rows, :LANES],
                flat[rows, LANES:],
            ]
        )

    info = map_ref[0].astype(f32)
    spread = mm(
        jnp.concatenate([jnp.where(same, info[i : i + 1], 0.0) for i in range(4)], axis=0),
        jnp.ones((slots, LANES), f32),
    ).astype(jnp.int32)
    owner, face, sub, orient = [spread[i * slots : (i + 1) * slots] for i in range(4)]
    half = jnp.where(iota((slots, LANES), 1) >= FN, 1, 0)
    upper = half == 1
    dim, end = face >> 1, face & 1

    high, low = split(
        jnp.concatenate(
            [jnp.concatenate([trace[v][d] for v in range(NV)], axis=1) for d in range(3)], axis=0
        )
    )
    rows = 3 * elems
    place = dim * elems + owner
    one_hot = jnp.where(place[:, : 2 * rows] == (iota((slots, 2 * rows), 1) % rows), 1.0, 0.0)
    picked = mm(one_hot, jnp.concatenate([high, low], axis=0))
    at_end = end == half
    parts = [
        jnp.where(at_end, picked[:, v * LANES : (v + 1) * LANES], 0.0) for v in range(NV)
    ]

    high, low = split(jnp.concatenate(parts, axis=0))
    turned = mm(
        jnp.concatenate([high, low], axis=1), jnp.concatenate([turn, turn], axis=0)
    )
    parts = chosen_turn(turned, orient, half)

    fetches[3].wait()
    quads = proj_ref[...].reshape(4 * FN, FN)
    quad_high, quad_low = split(quads)
    projected = mm_t(
        split_columns(parts, upper),
        jnp.concatenate([quad_high, quad_high, quad_low, jnp.zeros_like(quad_low)], axis=1),
    )
    native = chosen_quad(projected, parts, sub, half)
    native_heat = jnp.full((slots, LANES), heats[0], f32)
    for j in range(1, elems):
        native_heat = jnp.where(owner == j, heats[j], native_heat)

    for i in range(3):
        plane = jnp.where(upper, native[2 * i + 1], native[2 * i])
        send[:, i] = plane.reshape(blocks, TILE, LANES)
    send[:, 3] = native_heat.reshape(blocks, TILE, LANES)
    many = CAPS // TILE
    up_at, down_at = pl.ds(groups, many), pl.ds(groups + many, many)

    def to_peer(off):
        peer = lax.rem(grp + off, groups)
        return pltpu.make_async_remote_copy(
            src_ref=send.at[peer],
            dst_ref=recv.at[grp],
            send_sem=send_sem.at[off],
            recv_sem=recv_sem.at[off],
            device_id=(elem, peer),
            device_id_type=MESH,
        )

    def from_peer(off):
        peer = lax.rem(grp + groups - off, groups)
        return pltpu.make_async_remote_copy(
            src_ref=send.at[peer],
            dst_ref=recv.at[peer],
            send_sem=send_sem.at[off],
            recv_sem=recv_sem.at[off],
            device_id=(elem, peer),
            device_id_type=MESH,
        )

    def along(src, dst, sem, step):
        return pltpu.make_async_remote_copy(
            src_ref=send.at[src],
            dst_ref=recv.at[dst],
            send_sem=send_sem.at[sem],
            recv_sem=recv_sem.at[sem],
            device_id=(elem + step, grp),
            device_id_type=MESH,
        )

    up_sem, down_sem = groups, groups + 1
    pl.semaphore_wait(
        barrier, groups - 1 + has_up.astype(jnp.int32) + has_down.astype(jnp.int32)
    )

    @pl.when(has_up)
    def _():
        along(up_at, down_at, up_sem, 1).start()

    @pl.when(has_down)
    def _():
        along(down_at, up_at, down_sem, -1).start()

    for off in range(1, groups):
        to_peer(off).start()

    for fetch in fetches[4:]:
        fetch.wait()
    row8 = iota((TILE, LANES), 0)
    heat = jnp.full((TILE, LANES), heats[0], f32)
    for j in range(1, elems):
        heat = jnp.where(row8 == j, heats[j], heat)
    sign = jnp.where(upper8, 1.0, -1.0)
    across_all = nb_ref[...]
    local = []
    for d in range(3):
        across = jnp.where(
            upper8, across_all[:, 2 * d + 1 : 2 * d + 2], across_all[:, 2 * d : 2 * d + 1]
        )
        own = [trace[v][d] for v in range(NV)]
        opposite = [pltpu.roll(x, FN, 1) for x in own]
        other, other_heat = own, heat
        for j in range(elems):
            here = across == j
            other = [jnp.where(here, o[j : j + 1], x) for o, x in zip(opposite, other)]
            other_heat = jnp.where(here, heats[j], other_heat)
        normal = [None, None, None]
        normal[d] = sign
        jump = flux_jump(own, other, heat, other_heat, normal)
        local.append([jnp.where(across >= 0, x, 0.0) for x in jump])

    heat_all = jnp.concatenate([heat] * chunks, axis=1)
    inverse = 1.0 / u[0]
    velocity = [u[1 + d] * inverse for d in range(3)]
    kinetic = 0.5 * (u[1] * velocity[0] + u[2] * velocity[1] + u[3] * velocity[2])
    pressure = (heat_all - 1.0) * (u[4] - kinetic)

    def flux(d):
        s = velocity[d]
        f = [u[1 + d]] + [m * s for m in u[1:4]] + [(u[4] + pressure) * s, u[5] * s]
        f[1 + d] = f[1 + d] + pressure
        return f

    def cut(x):
        return [x[:, i * LANES : (i + 1) * LANES] for i in range(chunks)]

    deriv = cheb_matrix()
    flux_x, flux_y, flux_z = [[cut(f) for f in flux(d)] for d in range(3)]
    stacked = jnp.concatenate(
        [
            jnp.concatenate([flux_z[v][i], flux_y[v][i]], axis=1)
            for v in range(NV)
            for i in range(chunks)
        ],
        axis=0,
    )
    high, low = split(stacked)
    rows = NV * chunks * TILE
    both = mm(jnp.concatenate([high, low], axis=0), deriv_ref[...])
    plane_sum = both[:rows, :LANES] + both[:rows, LANES:] + both[rows:, :LANES]
    rolled_x = [[pltpu.roll(x, FN, 1) for x in flux_x[v]] for v in range(NV)]
    volume = [[None] * chunks for _ in range(NV)]
    for j in range(chunks):
        weights = []
        for i in range(chunks):
            straight = jnp.where(
                upper8, float(deriv[2 * j + 1, 2 * i + 1]), float(deriv[2 * j, 2 * i])
            )
            crossed = jnp.where(
                upper8, float(deriv[2 * j + 1, 2 * i]), float(deriv[2 * j, 2 * i + 1])
            )
            weights.append((straight, crossed))
        for v in range(NV):
            at = (v * chunks + j) * TILE
            total = plane_sum[at : at + TILE]
            for i in range(chunks):
                total = total + weights[i][0] * flux_x[v][i] + weights[i][1] * rolled_x[v][i]
            volume[v][j] = -total

    row = iota((TILE, LANES), 0)
    live = [row < count_ref[0, g] for g in range(groups)]
    for side_at in (groups, groups + 1):
        live += [row + TILE * i < count_ref[0, side_at] for i in range(many)]
    live = jnp.concatenate([jnp.where(x, 1.0, 0.0) for x in live], axis=0) > 0.0
    sign = jnp.where(end == 1, 1.0, -1.0)
    normal = [jnp.where(dim == d, sign, 0.0) for d in range(3)]
    back_weight = jnp.where(sub == 0, 1.0, 0.25)
    across_quads = jnp.concatenate([proj_ref[i] for i in range(4)], axis=1)
    quad_high, quad_low = split(across_quads)
    quads_back = jnp.concatenate(
        [quad_high, quad_high, quad_low, jnp.zeros_like(quad_low)], axis=0
    ).astype(bf16)
    back_orient = jnp.where(orient >= 5, jnp.where(orient == 7, 7, 11 - orient), orient)
    gather_at = (map_ref[0, 1:2, :] >> 1) * elems + map_ref[0, 0:1, :]
    gather = jnp.where(iota((3 * elems, slots), 0) == gather_at, 1.0, 0.0).astype(bf16)

    for off in range(1, groups):
        from_peer(off).wait_recv()

    @pl.when(has_up)
    def _():
        along(down_at, up_at, down_sem, 1).wait_recv()

    @pl.when(has_down)
    def _():
        along(up_at, down_at, up_sem, -1).wait_recv()

    partner = []
    for i in range(3):
        plane = recv[:, i].reshape(slots, LANES)
        moved = pltpu.roll(plane, FN, 1)
        partner += [jnp.where(upper, moved, plane), jnp.where(upper, plane, moved)]
    partner = [jnp.where(live, a, b) for a, b in zip(partner, native)]
    partner_heat = jnp.where(live, recv[:, 3].reshape(slots, LANES), native_heat)
    jump = flux_jump(native, partner, native_heat, partner_heat, normal)
    corr = [jnp.where(live, back_weight * x, 0.0) for x in jump]

    parts = chosen_quad(mm(split_columns(corr, upper), quads_back), corr, sub, half)
    lhs = []
    for x in parts:
        high, low = split(x)
        lhs.append(jnp.where(upper, low, high))
    parts = chosen_turn(mm(jnp.concatenate(lhs, axis=0), turn), back_orient, half)
    high, low = split(
        jnp.concatenate([jnp.where(at_end, x, 0.0) for x in parts], axis=1)
    )
    face_sum = mm(gather, high) + mm(gather, low)

    lines = []
    for v in range(NV):
        at = slice(v * LANES, (v + 1) * LANES)
        lines.append(
            [face_sum[d * elems : (d + 1) * elems, at] + local[d][v] for d in range(3)]
        )
    wide = jnp.concatenate([jnp.concatenate(x[1:], axis=1) for x in lines], axis=0)
    high, low = split(wide)
    both = mm_t(jnp.concatenate([high, low], axis=0), pick_nodes)
    surface = both[: NV * elems] + both[NV * elems :]
    scale = jnp.full((TILE, LANES), metric_ref[0], f32)
    for j in range(1, elems):
        scale = jnp.where(row8 == j, metric_ref[j], scale)
    scale = step_size * scale
    for v in range(NV):
        for j in range(chunks):
            s = surface[v * elems : (v + 1) * elems, j * LANES : (j + 1) * LANES]
            if j == 0:
                s = s + jnp.where(upper8, 0.0, lines[v][0])
            if j == chunks - 1:
                s = s + jnp.where(upper8, lines[v][0], 0.0)
            at = slice(j * LANES, (j + 1) * LANES)
            out_ref[v, :, at] = u[v][:, at] + scale * (volume[v][j] + lift_weight * s)

    for off in range(1, groups):
        to_peer(off).wait_send()

    @pl.when(has_up)
    def _():
        along(up_at, down_at, up_sem, 1).wait_send()

    @pl.when(has_down)
    def _():
        along(down_at, up_at, down_sem, -1).wait_send()


def shards(state, material, metric, mortar_proj, mortar_map, mortar_count, neighbours):
    groups, ranks = lax.axis_size("grp"), lax.axis_size("elem")
    blocks = mortar_map.shape[2] // TILE
    by_variable = jnp.transpose(state, (1, 0, 2))
    operands = (
        by_variable,
        mortar_map,
        material,
        mortar_proj,
        neighbours,
        mortar_count,
        metric,
        jnp.asarray(plane_derivative()),
    )
    in_smem = (2, 5, 6)
    result = pl.pallas_call(
        functools.partial(kernel, groups, ranks),
        out_shape=pltpu.VMEM(by_variable.shape, state.dtype),
        in_specs=[pl.BlockSpec(memory_space=pltpu.HBM)] * len(operands),
        out_specs=pl.BlockSpec(memory_space=pltpu.VMEM),
        scratch_shapes=[
            (pltpu.SMEM if i in in_smem else pltpu.VMEM)(x.shape, x.dtype)
            for i, x in enumerate(operands)
        ]
        + [
            pltpu.VMEM((blocks, 4, TILE, LANES), f32),
            pltpu.VMEM((blocks, 4, TILE, LANES), f32),
            pltpu.SemaphoreType.DMA((groups + 2,)),
            pltpu.SemaphoreType.DMA((groups + 2,)),
            pltpu.SemaphoreType.DMA((len(operands),)),
        ],
        compiler_params=pltpu.CompilerParams(
            collective_id=0, has_side_effects=True, vmem_limit_bytes=40 * 2**20
        ),
    )(*[pltpu.with_memory_space_constraint(x, pltpu.HBM) for x in operands])
    return jnp.transpose(result, (1, 0, 2))


def solution(mesh):
    return jax.shard_map(
        shards,
        mesh=mesh,
        in_specs=(
            P(("elem", "grp"), None, None),
            P(("elem", "grp")),
            P(("elem", "grp")),
            P(),
            P(("elem", "grp"), None, None),
            P(("elem", "grp"), None),
            P(("elem", "grp"), None),
        ),
        out_specs=P(("elem", "grp"), None, None),
        check_vma=False,
    )
```

```python
import functools

import jax
import jax.numpy as jnp
import numpy as np
from jax import lax
from jax.experimental import pallas as pl
from jax.experimental.pallas import tpu as pltpu
from jax.sharding import PartitionSpec as P

NV = 6
FN = 64
CAPG = 8
CAPS = 32
TILE = 8
LANES = 128

step_size = 0.002
lift_weight = 49.0
MESH = pl.DeviceIdType.MESH
f32 = jnp.float32
bf16 = jnp.bfloat16


def cheb_matrix():
    points = -np.cos(np.pi * np.arange(8) / 7.0)
    factor = np.array([2.0, 1.0, 1.0, 1.0, 1.0, 1.0, 1.0, 2.0])
    alternating = np.where(np.arange(8) % 2 == 0, 1.0, -1.0)
    scaled = factor * alternating
    differ = points[:, None] - points[None, :] + np.eye(8)
    matrix = scaled[:, None] / scaled[None, :] / differ
    matrix = matrix * (1.0 - np.eye(8))
    return matrix - np.eye(8) * matrix.sum(axis=1)[:, None]


def plane_derivative():
    deriv_t = cheb_matrix().astype(np.float32).T
    both = np.concatenate(
        [np.kron(np.eye(16), deriv_t), np.kron(np.eye(2), np.kron(deriv_t, np.eye(8)))], axis=0
    ).astype(np.float32)
    high = both.astype(bf16)
    low = (both - high.astype(np.float32)).astype(bf16)
    return np.concatenate([high, low], axis=1)


def iota(shape, dim):
    return lax.broadcasted_iota(jnp.int32, shape, dim)


def split(x):
    high = x.astype(bf16).astype(f32)
    return high, x - high


def mm(a, b):
    return lax.dot_general(
        a.astype(bf16), b.astype(bf16), (((1,), (0,)), ((), ())), preferred_element_type=f32
    )


def mm_t(a, b):
    return lax.dot_general(
        a.astype(bf16), b.astype(bf16), (((1,), (1,)), ((), ())), preferred_element_type=f32
    )


def side(u, heat, normal):
    inverse = 1.0 / u[0]
    through = sum(n * m for n, m in zip(normal, u[1:4]) if n is not None)
    speed = through * inverse
    kinetic = 0.5 * (u[1] * u[1] + u[2] * u[2] + u[3] * u[3]) * inverse
    pressure = (heat - 1.0) * (u[4] - kinetic)
    return speed, pressure, jnp.sqrt(heat * pressure * inverse)


def flux_jump(own, other, own_side, other_heat, normal):
    s_l, p_l, c_l = own_side
    s_r, p_r, c_r = side(other, other_heat, normal)
    wave_l = jnp.minimum(s_l - c_l, s_r - c_r)
    wave_r = jnp.maximum(s_l + c_l, s_r + c_r)
    mass_l = own[0] * (wave_l - s_l)
    mass_r = other[0] * (wave_r - s_r)
    middle = (p_r - p_l + mass_l * s_l - mass_r * s_r) / (mass_l - mass_r)
    left = jnp.logical_or(wave_l >= 0.0, middle >= 0.0)
    u = [jnp.where(left, a, b) for a, b in zip(own, other)]
    s = jnp.where(left, s_l, s_r)
    p = jnp.where(left, p_l, p_r)
    wave = jnp.where(left, wave_l, wave_r)
    active = jnp.where(left, jnp.minimum(wave_l, 0.0), jnp.maximum(wave_r, 0.0))
    shifted = middle - s
    growth = shifted / (wave - middle)
    lifted = active * (growth + 1.0) * shifted
    scale = s + active * growth
    push = p_l - p - lifted * u[0]
    work = p_l * s_l - p * s - lifted * (u[0] * middle + p / (wave - s))
    jump = [s_l * a - scale * b for a, b in zip(own, u)]
    for d in range(3):
        if normal[d] is not None:
            jump[1 + d] = jump[1 + d] + normal[d] * push
    jump[4] = jump[4] + work
    return jump


def chosen_turn(turned, orient, half):
    slots = orient.shape[0]
    pair = orient >> 1
    in_place = (orient & 1) == half
    result = []
    for v in range(NV):
        a, b, c, d = [
            turned[v * slots : (v + 1) * slots, i * LANES : (i + 1) * LANES] for i in range(4)
        ]
        x = jnp.where(pair == 0, a, jnp.where(pair == 1, b, jnp.where(pair == 2, c, d)))
        result.append(jnp.where(in_place, x, pltpu.roll(x, FN, 1)))
    return result


def split_columns(parts, upper):
    first, second = [], []
    for x in parts:
        high, low = split(x)
        first.append(jnp.where(upper, low, high))
        second.append(jnp.where(upper, 0.0, high))
    return jnp.concatenate(
        [jnp.concatenate(first, axis=0), jnp.concatenate(second, axis=0)], axis=1
    )


def chosen_quad(projected, parts, sub, half):
    slots = sub.shape[0]
    in_place = (sub & 1) != half
    result = []
    for v in range(NV):
        rows = slice(v * slots, (v + 1) * slots)
        x = jnp.where(sub >= 3, projected[rows, LANES:], projected[rows, :LANES])
        x = jnp.where(in_place, x, pltpu.roll(x, FN, 1))
        result.append(jnp.where(sub == 0, parts[v], x))
    return result


def kernel(
    groups,
    ranks,
    map_hbm,
    state_hbm,
    material_hbm,
    proj_hbm,
    nb_hbm,
    count_hbm,
    metric_hbm,
    deriv_hbm,
    out_ref,
    map_ref,
    state_ref,
    material_ref,
    proj_ref,
    nb_ref,
    count_ref,
    metric_ref,
    deriv_ref,
    send,
    recv,
    send_sem,
    recv_sem,
    fetch_sem,
):
    fetches = [
        pltpu.make_async_copy(src, dst, fetch_sem.at[i])
        for i, (src, dst) in enumerate(
            (
                (map_hbm, map_ref),
                (state_hbm, state_ref),
                (material_hbm, material_ref),
                (proj_hbm, proj_ref),
                (nb_hbm, nb_ref),
                (count_hbm, count_ref),
                (metric_hbm, metric_ref),
                (deriv_hbm, deriv_ref),
            )
        )
    ]
    for fetch in fetches[:4]:
        fetch.start()
    elem = lax.axis_index("elem")
    grp = lax.axis_index("grp")
    has_up = elem + 1 < ranks
    has_down = elem > 0
    barrier = pltpu.get_barrier_semaphore()
    for off in range(1, groups):
        pl.semaphore_signal(
            barrier, inc=1, device_id=(elem, lax.rem(grp + off, groups)), device_id_type=MESH
        )

    @pl.when(has_up)
    def _():
        pl.semaphore_signal(barrier, inc=1, device_id=(elem + 1, grp), device_id_type=MESH)

    @pl.when(has_down)
    def _():
        pl.semaphore_signal(barrier, inc=1, device_id=(elem - 1, grp), device_id_type=MESH)

    for fetch in fetches[4:]:
        fetch.start()
    slots = map_ref.shape[2]
    elems = state_ref.shape[1]
    nodes = state_ref.shape[2]
    blocks = slots // TILE
    chunks = nodes // LANES

    upper8 = iota((TILE, LANES), 1) >= FN
    col = iota((1, 256), 1)
    cell, far = col & 63, (col >> 6) & 1
    target = jnp.where(col < 128, 64 * (cell >> 3) + (cell & 7) + 56 * far, 8 * cell + 7 * far)
    pick_nodes = jnp.where(iota((nodes, 256), 0) == target, 1.0, 0.0).astype(bf16)
    col = iota((1, 512), 1)
    code, first, second = col >> 6, (col >> 3) & 7, col & 7
    swap = (code & 4) != 0
    first, second = jnp.where(swap, second, first), jnp.where(swap, first, second)
    first = jnp.where((code & 1) != 0, 7 - first, first)
    second = jnp.where((code & 2) != 0, 7 - second, second)
    turn = jnp.where((iota((LANES, 512), 0) & 63) == 8 * first + second, 1.0, 0.0).astype(bf16)
    same = iota((slots, slots), 0) == iota((slots, slots), 1)
    fetches[0].wait()
    info = map_ref[0].astype(f32)
    spread = mm(
        jnp.concatenate([jnp.where(same, info[i : i + 1], 0.0) for i in range(4)], axis=0),
        jnp.ones((slots, LANES), f32),
    ).astype(jnp.int32)
    owner, face, sub, orient = [spread[i * slots : (i + 1) * slots] for i in range(4)]
    half = jnp.where(iota((slots, LANES), 1) >= FN, 1, 0)
    upper = half == 1
    dim, end = face >> 1, face & 1
    at_end = end == half
    rows = 3 * elems
    place = dim * elems + owner
    one_hot = jnp.where(place[:, : 2 * rows] == (iota((slots, 2 * rows), 1) % rows), 1.0, 0.0).astype(bf16)

    for fetch in fetches[1:3]:
        fetch.wait()
    u = [state_ref[v] for v in range(NV)]
    heats = [1.4 + 0.27 * material_ref[j].astype(f32) for j in range(elems)]
    high, low = split(jnp.concatenate(u, axis=0))
    both = mm(jnp.concatenate([high, low], axis=0), pick_nodes)
    flat = both[: NV * elems] + both[NV * elems :]
    trace = []
    for v in range(NV):
        rows = slice(v * elems, (v + 1) * elems)
        trace.append(
            [
                jnp.where(upper8, u[v][:, nodes - LANES :], u[v][:, :LANES]),
                flat[rows, :LANES],
                flat[rows, LANES:],
            ]
        )

    high, low = split(
        jnp.concatenate(
            [jnp.concatenate([trace[v][d] for v in range(NV)], axis=1) for d in range(3)], axis=0
        )
    )
    picked = mm(one_hot, jnp.concatenate([high, low], axis=0))
    parts = [
        jnp.where(at_end, picked[:, v * LANES : (v + 1) * LANES], 0.0) for v in range(NV)
    ]

    high, low = split(jnp.concatenate(parts, axis=0))
    turned = mm(
        jnp.concatenate([high, low], axis=1), jnp.concatenate([turn, turn], axis=0)
    )
    parts = chosen_turn(turned, orient, half)

    fetches[3].wait()
    quads = proj_ref[...].reshape(4 * FN, FN)
    quad_high, quad_low = split(quads)
    projected = mm_t(
        split_columns(parts, upper),
        jnp.concatenate([quad_high, quad_high, quad_low, jnp.zeros_like(quad_low)], axis=1),
    )
    native = chosen_quad(projected, parts, sub, half)
    native_heat = jnp.full((slots, LANES), heats[0], f32)
    for j in range(1, elems):
        native_heat = jnp.where(owner == j, heats[j], native_heat)

    for i in range(3):
        plane = jnp.where(upper, native[2 * i + 1], native[2 * i])
        send[:, i] = plane.reshape(blocks, TILE, LANES)
    send[:, 3] = native_heat.reshape(blocks, TILE, LANES)
    many = CAPS // TILE
    up_at, down_at = pl.ds(groups, many), pl.ds(groups + many, many)

    def to_peer(off):
        peer = lax.rem(grp + off, groups)
        return pltpu.make_async_remote_copy(
            src_ref=send.at[peer],
            dst_ref=recv.at[grp],
            send_sem=send_sem.at[off],
            recv_sem=recv_sem.at[off],
            device_id=(elem, peer),
            device_id_type=MESH,
        )

    def from_peer(off):
        peer = lax.rem(grp + groups - off, groups)
        return pltpu.make_async_remote_copy(
            src_ref=send.at[peer],
            dst_ref=recv.at[peer],
            send_sem=send_sem.at[off],
            recv_sem=recv_sem.at[off],
            device_id=(elem, peer),
            device_id_type=MESH,
        )

    def along(src, dst, sem, step):
        return pltpu.make_async_remote_copy(
            src_ref=send.at[src],
            dst_ref=recv.at[dst],
            send_sem=send_sem.at[sem],
            recv_sem=recv_sem.at[sem],
            device_id=(elem + step, grp),
            device_id_type=MESH,
        )

    up_sem, down_sem = groups, groups + 1
    pl.semaphore_wait(
        barrier, groups - 1 + has_up.astype(jnp.int32) + has_down.astype(jnp.int32)
    )

    @pl.when(has_up)
    def _():
        along(up_at, down_at, up_sem, 1).start()

    @pl.when(has_down)
    def _():
        along(down_at, up_at, down_sem, -1).start()

    for off in range(1, groups):
        to_peer(off).start()

    for fetch in fetches[4:]:
        fetch.wait()
    row8 = iota((TILE, LANES), 0)
    heat = jnp.full((TILE, LANES), heats[0], f32)
    for j in range(1, elems):
        heat = jnp.where(row8 == j, heats[j], heat)
    sign = jnp.where(upper8, 1.0, -1.0)
    across_all = nb_ref[...]
    local = []
    for d in range(3):
        across = jnp.where(
            upper8, across_all[:, 2 * d + 1 : 2 * d + 2], across_all[:, 2 * d : 2 * d + 1]
        )
        own = [trace[v][d] for v in range(NV)]
        opposite = [pltpu.roll(x, FN, 1) for x in own]
        other, other_heat = own, heat
        for j in range(elems):
            here = across == j
            other = [jnp.where(here, o[j : j + 1], x) for o, x in zip(opposite, other)]
            other_heat = jnp.where(here, heats[j], other_heat)
        normal = [None, None, None]
        normal[d] = sign
        jump = flux_jump(own, other, side(own, heat, normal), other_heat, normal)
        local.append([jnp.where(across >= 0, x, 0.0) for x in jump])

    heat_all = jnp.concatenate([heat] * chunks, axis=1)
    inverse = 1.0 / u[0]
    velocity = [u[1 + d] * inverse for d in range(3)]
    kinetic = 0.5 * (u[1] * velocity[0] + u[2] * velocity[1] + u[3] * velocity[2])
    pressure = (heat_all - 1.0) * (u[4] - kinetic)

    def flux(d):
        s = velocity[d]
        f = [u[1 + d]] + [m * s for m in u[1:4]] + [(u[4] + pressure) * s, u[5] * s]
        f[1 + d] = f[1 + d] + pressure
        return f

    def cut(x):
        return [x[:, i * LANES : (i + 1) * LANES] for i in range(chunks)]

    deriv = cheb_matrix()
    flux_x, flux_y, flux_z = [[cut(f) for f in flux(d)] for d in range(3)]
    stacked = jnp.concatenate(
        [
            jnp.concatenate([flux_z[v][i], flux_y[v][i]], axis=1)
            for v in range(NV)
            for i in range(chunks)
        ],
        axis=0,
    )
    high, low = split(stacked)
    rows = NV * chunks * TILE
    both = mm(jnp.concatenate([high, low], axis=0), deriv_ref[...])
    plane_sum = both[:rows, :LANES] + both[:rows, LANES:] + both[rows:, :LANES]
    rolled_x = [[pltpu.roll(x, FN, 1) for x in flux_x[v]] for v in range(NV)]
    volume = [[None] * chunks for _ in range(NV)]
    for j in range(chunks):
        weights = []
        for i in range(chunks):
            straight = jnp.where(
                upper8, float(deriv[2 * j + 1, 2 * i + 1]), float(deriv[2 * j, 2 * i])
            )
            crossed = jnp.where(
                upper8, float(deriv[2 * j + 1, 2 * i]), float(deriv[2 * j, 2 * i + 1])
            )
            weights.append((straight, crossed))
        for v in range(NV):
            at = (v * chunks + j) * TILE
            total = plane_sum[at : at + TILE]
            for i in range(chunks):
                total = total + weights[i][0] * flux_x[v][i] + weights[i][1] * rolled_x[v][i]
            volume[v][j] = -total

    row = iota((TILE, LANES), 0)
    live = [row < count_ref[0, g] for g in range(groups)]
    for side_at in (groups, groups + 1):
        live += [row + TILE * i < count_ref[0, side_at] for i in range(many)]
    live = jnp.concatenate([jnp.where(x, 1.0, 0.0) for x in live], axis=0) > 0.0
    sign = jnp.where(end == 1, 1.0, -1.0)
    normal = [jnp.where(dim == d, sign, 0.0) for d in range(3)]
    back_weight = jnp.where(sub == 0, 1.0, 0.25)
    across_quads = jnp.concatenate([proj_ref[i] for i in range(4)], axis=1)
    quad_high, quad_low = split(across_quads)
    quads_back = jnp.concatenate(
        [quad_high, quad_high, quad_low, jnp.zeros_like(quad_low)], axis=0
    ).astype(bf16)
    back_orient = jnp.where(orient >= 5, jnp.where(orient == 7, 7, 11 - orient), orient)
    gather_at = (map_ref[0, 1:2, :] >> 1) * elems + map_ref[0, 0:1, :]
    gather = jnp.where(iota((3 * elems, slots), 0) == gather_at, 1.0, 0.0).astype(bf16)

    native_side = side(native, native_heat, normal)
    scale = jnp.full((TILE, LANES), metric_ref[0], f32)
    for j in range(1, elems):
        scale = jnp.where(row8 == j, metric_ref[j], scale)
    scale = step_size * scale
    base = [
        [u[v][:, j * LANES : (j + 1) * LANES] + scale * volume[v][j] for j in range(chunks)]
        for v in range(NV)
    ]
    scale = lift_weight * scale

    for off in range(1, groups):
        from_peer(off).wait_recv()

    @pl.when(has_up)
    def _():
        along(down_at, up_at, down_sem, 1).wait_recv()

    @pl.when(has_down)
    def _():
        along(up_at, down_at, up_sem, -1).wait_recv()

    partner = []
    for i in range(3):
        plane = recv[:, i].reshape(slots, LANES)
        moved = pltpu.roll(plane, FN, 1)
        partner += [jnp.where(upper, moved, plane), jnp.where(upper, plane, moved)]
    partner = [jnp.where(live, a, b) for a, b in zip(partner, native)]
    partner_heat = jnp.where(live, recv[:, 3].reshape(slots, LANES), native_heat)
    jump = flux_jump(native, partner, native_side, partner_heat, normal)
    corr = [jnp.where(live, back_weight * x, 0.0) for x in jump]

    parts = chosen_quad(mm(split_columns(corr, upper), quads_back), corr, sub, half)
    lhs = []
    for x in parts:
        high, low = split(x)
        lhs.append(jnp.where(upper, low, high))
    parts = chosen_turn(mm(jnp.concatenate(lhs, axis=0), turn), back_orient, half)
    high, low = split(
        jnp.concatenate([jnp.where(at_end, x, 0.0) for x in parts], axis=1)
    )
    face_sum = mm(gather, high) + mm(gather, low)

    lines = []
    for v in range(NV):
        at = slice(v * LANES, (v + 1) * LANES)
        lines.append(
            [face_sum[d * elems : (d + 1) * elems, at] + local[d][v] for d in range(3)]
        )
    wide = jnp.concatenate([jnp.concatenate(x[1:], axis=1) for x in lines], axis=0)
    high, low = split(wide)
    both = mm_t(jnp.concatenate([high, low], axis=0), pick_nodes)
    surface = both[: NV * elems] + both[NV * elems :]
    for v in range(NV):
        for j in range(chunks):
            s = surface[v * elems : (v + 1) * elems, j * LANES : (j + 1) * LANES]
            if j == 0:
                s = s + jnp.where(upper8, 0.0, lines[v][0])
            if j == chunks - 1:
                s = s + jnp.where(upper8, lines[v][0], 0.0)
            at = slice(j * LANES, (j + 1) * LANES)
            out_ref[v, :, at] = base[v][j] + scale * s

    for off in range(1, groups):
        to_peer(off).wait_send()

    @pl.when(has_up)
    def _():
        along(up_at, down_at, up_sem, 1).wait_send()

    @pl.when(has_down)
    def _():
        along(down_at, up_at, down_sem, -1).wait_send()


def shards(state, material, metric, mortar_proj, mortar_map, mortar_count, neighbours):
    groups, ranks = lax.axis_size("grp"), lax.axis_size("elem")
    blocks = mortar_map.shape[2] // TILE
    by_variable = jnp.transpose(state, (1, 0, 2))
    operands = (
        mortar_map,
        by_variable,
        material,
        mortar_proj,
        neighbours,
        mortar_count,
        metric,
        jnp.asarray(plane_derivative()),
    )
    in_smem = (2, 5, 6)
    result = pl.pallas_call(
        functools.partial(kernel, groups, ranks),
        out_shape=pltpu.VMEM(by_variable.shape, state.dtype),
        in_specs=[pl.BlockSpec(memory_space=pltpu.HBM)] * len(operands),
        out_specs=pl.BlockSpec(memory_space=pltpu.VMEM),
        scratch_shapes=[
            (pltpu.SMEM if i in in_smem else pltpu.VMEM)(x.shape, x.dtype)
            for i, x in enumerate(operands)
        ]
        + [
            pltpu.VMEM((blocks, 4, TILE, LANES), f32),
            pltpu.VMEM((blocks, 4, TILE, LANES), f32),
            pltpu.SemaphoreType.DMA((groups + 2,)),
            pltpu.SemaphoreType.DMA((groups + 2,)),
            pltpu.SemaphoreType.DMA((len(operands),)),
        ],
        compiler_params=pltpu.CompilerParams(
            collective_id=0, has_side_effects=True, vmem_limit_bytes=40 * 2**20
        ),
    )(*[pltpu.with_memory_space_constraint(x, pltpu.HBM) for x in operands])
    return jnp.transpose(result, (1, 0, 2))


def solution(mesh):
    return jax.shard_map(
        shards,
        mesh=mesh,
        in_specs=(
            P(("elem", "grp"), None, None),
            P(("elem", "grp")),
            P(("elem", "grp")),
            P(),
            P(("elem", "grp"), None, None),
            P(("elem", "grp"), None),
            P(("elem", "grp"), None),
        ),
        out_specs=P(("elem", "grp"), None, None),
        check_vma=False,
    )
```

```python
import functools

import jax
import jax.numpy as jnp
import numpy as np
from jax import lax
from jax.experimental import pallas as pl
from jax.experimental.pallas import tpu as pltpu
from jax.sharding import PartitionSpec as P

NV = 6
FN = 64
CAPG = 8
CAPS = 32
TILE = 8
LANES = 128

step_size = 0.002
lift_weight = 49.0
MESH = pl.DeviceIdType.MESH
f32 = jnp.float32
bf16 = jnp.bfloat16


def cheb_matrix():
    points = -np.cos(np.pi * np.arange(8) / 7.0)
    factor = np.array([2.0, 1.0, 1.0, 1.0, 1.0, 1.0, 1.0, 2.0])
    alternating = np.where(np.arange(8) % 2 == 0, 1.0, -1.0)
    scaled = factor * alternating
    differ = points[:, None] - points[None, :] + np.eye(8)
    matrix = scaled[:, None] / scaled[None, :] / differ
    matrix = matrix * (1.0 - np.eye(8))
    return matrix - np.eye(8) * matrix.sum(axis=1)[:, None]


def plane_derivative():
    deriv_t = cheb_matrix().astype(np.float32).T
    both = np.concatenate(
        [np.kron(np.eye(16), deriv_t), np.kron(np.eye(2), np.kron(deriv_t, np.eye(8)))], axis=0
    ).astype(np.float32)
    high = both.astype(bf16)
    low = (both - high.astype(np.float32)).astype(bf16)
    return np.concatenate([high, low], axis=1)


def iota(shape, dim):
    return lax.broadcasted_iota(jnp.int32, shape, dim)


def split(x):
    high = x.astype(bf16).astype(f32)
    return high, x - high


def mm(a, b):
    return lax.dot_general(
        a.astype(bf16), b.astype(bf16), (((1,), (0,)), ((), ())), preferred_element_type=f32
    )


def mm_t(a, b):
    return lax.dot_general(
        a.astype(bf16), b.astype(bf16), (((1,), (1,)), ((), ())), preferred_element_type=f32
    )


def side(u, heat, normal):
    inverse = 1.0 / u[0]
    through = sum(n * m for n, m in zip(normal, u[1:4]) if n is not None)
    speed = through * inverse
    kinetic = 0.5 * (u[1] * u[1] + u[2] * u[2] + u[3] * u[3]) * inverse
    pressure = (heat - 1.0) * (u[4] - kinetic)
    return speed, pressure, jnp.sqrt(heat * pressure * inverse)


def flux_jump(own, other, own_side, other_heat, normal):
    s_l, p_l, c_l = own_side
    s_r, p_r, c_r = side(other, other_heat, normal)
    wave_l = jnp.minimum(s_l - c_l, s_r - c_r)
    wave_r = jnp.maximum(s_l + c_l, s_r + c_r)
    mass_l = own[0] * (wave_l - s_l)
    mass_r = other[0] * (wave_r - s_r)
    middle = (p_r - p_l + mass_l * s_l - mass_r * s_r) / (mass_l - mass_r)
    left = jnp.logical_or(wave_l >= 0.0, middle >= 0.0)
    u = [jnp.where(left, a, b) for a, b in zip(own, other)]
    s = jnp.where(left, s_l, s_r)
    p = jnp.where(left, p_l, p_r)
    wave = jnp.where(left, wave_l, wave_r)
    active = jnp.where(left, jnp.minimum(wave_l, 0.0), jnp.maximum(wave_r, 0.0))
    shifted = middle - s
    growth = shifted / (wave - middle)
    lifted = active * (growth + 1.0) * shifted
    scale = s + active * growth
    push = p_l - p - lifted * u[0]
    work = p_l * s_l - p * s - lifted * (u[0] * middle + p / (wave - s))
    jump = [s_l * a - scale * b for a, b in zip(own, u)]
    for d in range(3):
        if normal[d] is not None:
            jump[1 + d] = jump[1 + d] + normal[d] * push
    jump[4] = jump[4] + work
    return jump


def chosen_turn(turned, orient, half):
    slots = orient.shape[0]
    pair = orient >> 1
    in_place = (orient & 1) == half
    result = []
    for v in range(NV):
        a, b, c, d = [
            turned[v * slots : (v + 1) * slots, i * LANES : (i + 1) * LANES] for i in range(4)
        ]
        x = jnp.where(pair == 0, a, jnp.where(pair == 1, b, jnp.where(pair == 2, c, d)))
        result.append(jnp.where(in_place, x, pltpu.roll(x, FN, 1)))
    return result


def split_columns(parts, upper):
    first, second = [], []
    for x in parts:
        high, low = split(x)
        first.append(jnp.where(upper, low, high))
        second.append(jnp.where(upper, 0.0, high))
    return jnp.concatenate(
        [jnp.concatenate(first, axis=0), jnp.concatenate(second, axis=0)], axis=1
    )


def chosen_quad(projected, parts, sub, half):
    slots = sub.shape[0]
    in_place = (sub & 1) != half
    result = []
    for v in range(NV):
        rows = slice(v * slots, (v + 1) * slots)
        x = jnp.where(sub >= 3, projected[rows, LANES:], projected[rows, :LANES])
        x = jnp.where(in_place, x, pltpu.roll(x, FN, 1))
        result.append(jnp.where(sub == 0, parts[v], x))
    return result


def kernel(
    groups,
    ranks,
    map_hbm,
    state_hbm,
    material_hbm,
    proj_hbm,
    nb_hbm,
    count_hbm,
    metric_hbm,
    deriv_hbm,
    out_ref,
    map_ref,
    state_ref,
    material_ref,
    proj_ref,
    nb_ref,
    count_ref,
    metric_ref,
    deriv_ref,
    send,
    recv,
    send_sem,
    recv_sem,
    fetch_sem,
):
    fetches = [
        pltpu.make_async_copy(src, dst, fetch_sem.at[i])
        for i, (src, dst) in enumerate(
            (
                (map_hbm, map_ref),
                (state_hbm, state_ref),
                (material_hbm, material_ref),
                (proj_hbm, proj_ref),
                (nb_hbm, nb_ref),
                (count_hbm, count_ref),
                (metric_hbm, metric_ref),
                (deriv_hbm, deriv_ref),
            )
        )
    ]
    for fetch in fetches[:4]:
        fetch.start()
    elem = lax.axis_index("elem")
    grp = lax.axis_index("grp")
    has_up = elem + 1 < ranks
    has_down = elem > 0
    barrier = pltpu.get_barrier_semaphore()
    for off in range(1, groups):
        pl.semaphore_signal(
            barrier, inc=1, device_id=(elem, lax.rem(grp + off, groups)), device_id_type=MESH
        )

    @pl.when(has_up)
    def _():
        pl.semaphore_signal(barrier, inc=1, device_id=(elem + 1, grp), device_id_type=MESH)

    @pl.when(has_down)
    def _():
        pl.semaphore_signal(barrier, inc=1, device_id=(elem - 1, grp), device_id_type=MESH)

    for fetch in fetches[4:]:
        fetch.start()
    slots = map_ref.shape[2]
    elems = state_ref.shape[1]
    nodes = state_ref.shape[2]
    blocks = slots // TILE
    chunks = nodes // LANES

    upper8 = iota((TILE, LANES), 1) >= FN
    col = iota((1, 256), 1)
    cell, far = col & 63, (col >> 6) & 1
    target = jnp.where(col < 128, 64 * (cell >> 3) + (cell & 7) + 56 * far, 8 * cell + 7 * far)
    pick_nodes = jnp.where(iota((nodes, 256), 0) == target, 1.0, 0.0).astype(bf16)
    col = iota((1, 512), 1)
    code, first, second = col >> 6, (col >> 3) & 7, col & 7
    swap = (code & 4) != 0
    first, second = jnp.where(swap, second, first), jnp.where(swap, first, second)
    first = jnp.where((code & 1) != 0, 7 - first, first)
    second = jnp.where((code & 2) != 0, 7 - second, second)
    turn = jnp.where((iota((LANES, 512), 0) & 63) == 8 * first + second, 1.0, 0.0).astype(bf16)
    same = iota((slots, slots), 0) == iota((slots, slots), 1)
    fetches[0].wait()
    info = map_ref[0].astype(f32)
    spread = mm(
        jnp.concatenate([jnp.where(same, info[i : i + 1], 0.0) for i in range(4)], axis=0),
        jnp.ones((slots, LANES), f32),
    ).astype(jnp.int32)
    owner, face, sub, orient = [spread[i * slots : (i + 1) * slots] for i in range(4)]
    half = jnp.where(iota((slots, LANES), 1) >= FN, 1, 0)
    upper = half == 1
    dim, end = face >> 1, face & 1
    at_end = end == half
    rows = 3 * elems
    place = dim * elems + owner
    one_hot = jnp.where(place[:, : 2 * rows] == (iota((slots, 2 * rows), 1) % rows), 1.0, 0.0).astype(bf16)

    for fetch in fetches[1:3]:
        fetch.wait()
    u = [state_ref[v] for v in range(NV)]
    heats = [1.4 + 0.27 * material_ref[j].astype(f32) for j in range(elems)]
    high, low = split(jnp.concatenate(u, axis=0))
    both = mm(jnp.concatenate([high, low], axis=0), pick_nodes)
    flat = both[: NV * elems] + both[NV * elems :]
    trace = []
    for v in range(NV):
        rows = slice(v * elems, (v + 1) * elems)
        trace.append(
            [
                jnp.where(upper8, u[v][:, nodes - LANES :], u[v][:, :LANES]),
                flat[rows, :LANES],
                flat[rows, LANES:],
            ]
        )

    high, low = split(
        jnp.concatenate(
            [jnp.concatenate([trace[v][d] for v in range(NV)], axis=1) for d in range(3)], axis=0
        )
    )
    by_place = jnp.concatenate([high, low], axis=0).astype(bf16)
    turn_twice = jnp.concatenate([turn, turn], axis=0)
    fetches[3].wait()
    quads = proj_ref[...].reshape(4 * FN, FN)
    quad_high, quad_low = split(quads)
    quads_out = jnp.concatenate(
        [quad_high, quad_high, quad_low, jnp.zeros_like(quad_low)], axis=1
    ).astype(bf16)

    def mortar_traces(at):
        picked = mm(one_hot[at], by_place)
        parts = [
            jnp.where(at_end[at], picked[:, v * LANES : (v + 1) * LANES], 0.0) for v in range(NV)
        ]
        high, low = split(jnp.concatenate(parts, axis=0))
        turned = mm(jnp.concatenate([high, low], axis=1), turn_twice)
        parts = chosen_turn(turned, orient[at], half[at])
        projected = mm_t(split_columns(parts, upper[at]), quads_out)
        parts = chosen_quad(projected, parts, sub[at], half[at])
        tiles = slice(at.start // TILE, at.stop // TILE)
        for i in range(3):
            plane = jnp.where(upper[at], parts[2 * i + 1], parts[2 * i])
            send[tiles, i] = plane.reshape(-1, TILE, LANES)
        send[tiles, 3] = native_heat[at].reshape(-1, TILE, LANES)
        return parts

    native_heat = jnp.full((slots, LANES), heats[0], f32)
    for j in range(1, elems):
        native_heat = jnp.where(owner == j, heats[j], native_heat)

    many = CAPS // TILE
    up_at, down_at = pl.ds(groups, many), pl.ds(groups + many, many)

    def to_peer(off):
        peer = lax.rem(grp + off, groups)
        return pltpu.make_async_remote_copy(
            src_ref=send.at[peer],
            dst_ref=recv.at[grp],
            send_sem=send_sem.at[off],
            recv_sem=recv_sem.at[off],
            device_id=(elem, peer),
            device_id_type=MESH,
        )

    def from_peer(off):
        peer = lax.rem(grp + groups - off, groups)
        return pltpu.make_async_remote_copy(
            src_ref=send.at[peer],
            dst_ref=recv.at[peer],
            send_sem=send_sem.at[off],
            recv_sem=recv_sem.at[off],
            device_id=(elem, peer),
            device_id_type=MESH,
        )

    def along(src, dst, sem, step):
        return pltpu.make_async_remote_copy(
            src_ref=send.at[src],
            dst_ref=recv.at[dst],
            send_sem=send_sem.at[sem],
            recv_sem=recv_sem.at[sem],
            device_id=(elem + step, grp),
            device_id_type=MESH,
        )

    up_sem, down_sem = groups, groups + 1
    elem_native = mortar_traces(slice(groups * CAPG, slots))
    pl.semaphore_wait(
        barrier, groups - 1 + has_up.astype(jnp.int32) + has_down.astype(jnp.int32)
    )

    @pl.when(has_up)
    def _():
        along(up_at, down_at, up_sem, 1).start()

    @pl.when(has_down)
    def _():
        along(down_at, up_at, down_sem, -1).start()

    grp_native = mortar_traces(slice(0, groups * CAPG))
    for off in range(1, groups):
        to_peer(off).start()
    native = [jnp.concatenate(x, axis=0) for x in zip(grp_native, elem_native)]

    for fetch in fetches[4:]:
        fetch.wait()
    row8 = iota((TILE, LANES), 0)
    heat = jnp.full((TILE, LANES), heats[0], f32)
    for j in range(1, elems):
        heat = jnp.where(row8 == j, heats[j], heat)
    sign = jnp.where(upper8, 1.0, -1.0)
    across_all = nb_ref[...]
    local = []
    for d in range(3):
        across = jnp.where(
            upper8, across_all[:, 2 * d + 1 : 2 * d + 2], across_all[:, 2 * d : 2 * d + 1]
        )
        own = [trace[v][d] for v in range(NV)]
        opposite = [pltpu.roll(x, FN, 1) for x in own]
        other, other_heat = own, heat
        for j in range(elems):
            here = across == j
            other = [jnp.where(here, o[j : j + 1], x) for o, x in zip(opposite, other)]
            other_heat = jnp.where(here, heats[j], other_heat)
        normal = [None, None, None]
        normal[d] = sign
        jump = flux_jump(own, other, side(own, heat, normal), other_heat, normal)
        local.append([jnp.where(across >= 0, x, 0.0) for x in jump])

    heat_all = jnp.concatenate([heat] * chunks, axis=1)
    inverse = 1.0 / u[0]
    velocity = [u[1 + d] * inverse for d in range(3)]
    kinetic = 0.5 * (u[1] * velocity[0] + u[2] * velocity[1] + u[3] * velocity[2])
    pressure = (heat_all - 1.0) * (u[4] - kinetic)

    def flux(d):
        s = velocity[d]
        f = [u[1 + d]] + [m * s for m in u[1:4]] + [(u[4] + pressure) * s, u[5] * s]
        f[1 + d] = f[1 + d] + pressure
        return f

    def cut(x):
        return [x[:, i * LANES : (i + 1) * LANES] for i in range(chunks)]

    deriv = cheb_matrix()
    flux_x, flux_y, flux_z = [[cut(f) for f in flux(d)] for d in range(3)]
    stacked = jnp.concatenate(
        [
            jnp.concatenate([flux_z[v][i], flux_y[v][i]], axis=1)
            for v in range(NV)
            for i in range(chunks)
        ],
        axis=0,
    )
    high, low = split(stacked)
    rows = NV * chunks * TILE
    both = mm(jnp.concatenate([high, low], axis=0), deriv_ref[...])
    plane_sum = both[:rows, :LANES] + both[:rows, LANES:] + both[rows:, :LANES]
    rolled_x = [[pltpu.roll(x, FN, 1) for x in flux_x[v]] for v in range(NV)]
    volume = [[None] * chunks for _ in range(NV)]
    for j in range(chunks):
        weights = []
        for i in range(chunks):
            straight = jnp.where(
                upper8, float(deriv[2 * j + 1, 2 * i + 1]), float(deriv[2 * j, 2 * i])
            )
            crossed = jnp.where(
                upper8, float(deriv[2 * j + 1, 2 * i]), float(deriv[2 * j, 2 * i + 1])
            )
            weights.append((straight, crossed))
        for v in range(NV):
            at = (v * chunks + j) * TILE
            total = plane_sum[at : at + TILE]
            for i in range(chunks):
                total = total + weights[i][0] * flux_x[v][i] + weights[i][1] * rolled_x[v][i]
            volume[v][j] = -total

    row = iota((TILE, LANES), 0)
    live = [row < count_ref[0, g] for g in range(groups)]
    for side_at in (groups, groups + 1):
        live += [row + TILE * i < count_ref[0, side_at] for i in range(many)]
    live = jnp.concatenate([jnp.where(x, 1.0, 0.0) for x in live], axis=0) > 0.0
    sign = jnp.where(end == 1, 1.0, -1.0)
    normal = [jnp.where(dim == d, sign, 0.0) for d in range(3)]
    back_weight = jnp.where(sub == 0, 1.0, 0.25)
    across_quads = jnp.concatenate([proj_ref[i] for i in range(4)], axis=1)
    quad_high, quad_low = split(across_quads)
    quads_back = jnp.concatenate(
        [quad_high, quad_high, quad_low, jnp.zeros_like(quad_low)], axis=0
    ).astype(bf16)
    back_orient = jnp.where(orient >= 5, jnp.where(orient == 7, 7, 11 - orient), orient)
    gather_at = (map_ref[0, 1:2, :] >> 1) * elems + map_ref[0, 0:1, :]
    gather = jnp.where(iota((3 * elems, slots), 0) == gather_at, 1.0, 0.0).astype(bf16)

    native_side = side(native, native_heat, normal)
    scale = jnp.full((TILE, LANES), metric_ref[0], f32)
    for j in range(1, elems):
        scale = jnp.where(row8 == j, metric_ref[j], scale)
    scale = step_size * scale
    base = [
        [u[v][:, j * LANES : (j + 1) * LANES] + scale * volume[v][j] for j in range(chunks)]
        for v in range(NV)
    ]
    scale = lift_weight * scale

    for off in range(1, groups):
        from_peer(off).wait_recv()

    @pl.when(has_up)
    def _():
        along(down_at, up_at, down_sem, 1).wait_recv()

    @pl.when(has_down)
    def _():
        along(up_at, down_at, up_sem, -1).wait_recv()

    partner = []
    for i in range(3):
        plane = recv[:, i].reshape(slots, LANES)
        moved = pltpu.roll(plane, FN, 1)
        partner += [jnp.where(upper, moved, plane), jnp.where(upper, plane, moved)]
    partner = [jnp.where(live, a, b) for a, b in zip(partner, native)]
    partner_heat = jnp.where(live, recv[:, 3].reshape(slots, LANES), native_heat)
    jump = flux_jump(native, partner, native_side, partner_heat, normal)
    corr = [jnp.where(live, back_weight * x, 0.0) for x in jump]

    parts = chosen_quad(mm(split_columns(corr, upper), quads_back), corr, sub, half)
    lhs = []
    for x in parts:
        high, low = split(x)
        lhs.append(jnp.where(upper, low, high))
    parts = chosen_turn(mm(jnp.concatenate(lhs, axis=0), turn), back_orient, half)
    high, low = split(
        jnp.concatenate([jnp.where(at_end, x, 0.0) for x in parts], axis=1)
    )
    face_sum = mm(gather, high) + mm(gather, low)

    lines = []
    for v in range(NV):
        at = slice(v * LANES, (v + 1) * LANES)
        lines.append(
            [face_sum[d * elems : (d + 1) * elems, at] + local[d][v] for d in range(3)]
        )
    wide = jnp.concatenate([jnp.concatenate(x[1:], axis=1) for x in lines], axis=0)
    high, low = split(wide)
    both = mm_t(jnp.concatenate([high, low], axis=0), pick_nodes)
    surface = both[: NV * elems] + both[NV * elems :]
    for v in range(NV):
        for j in range(chunks):
            s = surface[v * elems : (v + 1) * elems, j * LANES : (j + 1) * LANES]
            if j == 0:
                s = s + jnp.where(upper8, 0.0, lines[v][0])
            if j == chunks - 1:
                s = s + jnp.where(upper8, lines[v][0], 0.0)
            at = slice(j * LANES, (j + 1) * LANES)
            out_ref[v, :, at] = base[v][j] + scale * s

    for off in range(1, groups):
        to_peer(off).wait_send()

    @pl.when(has_up)
    def _():
        along(up_at, down_at, up_sem, 1).wait_send()

    @pl.when(has_down)
    def _():
        along(down_at, up_at, down_sem, -1).wait_send()


def shards(state, material, metric, mortar_proj, mortar_map, mortar_count, neighbours):
    groups, ranks = lax.axis_size("grp"), lax.axis_size("elem")
    blocks = mortar_map.shape[2] // TILE
    by_variable = jnp.transpose(state, (1, 0, 2))
    operands = (
        mortar_map,
        by_variable,
        material,
        mortar_proj,
        neighbours,
        mortar_count,
        metric,
        jnp.asarray(plane_derivative()),
    )
    in_smem = (2, 5, 6)
    result = pl.pallas_call(
        functools.partial(kernel, groups, ranks),
        out_shape=pltpu.VMEM(by_variable.shape, state.dtype),
        in_specs=[pl.BlockSpec(memory_space=pltpu.HBM)] * len(operands),
        out_specs=pl.BlockSpec(memory_space=pltpu.VMEM),
        scratch_shapes=[
            (pltpu.SMEM if i in in_smem else pltpu.VMEM)(x.shape, x.dtype)
            for i, x in enumerate(operands)
        ]
        + [
            pltpu.VMEM((blocks, 4, TILE, LANES), f32),
            pltpu.VMEM((blocks, 4, TILE, LANES), f32),
            pltpu.SemaphoreType.DMA((groups + 2,)),
            pltpu.SemaphoreType.DMA((groups + 2,)),
            pltpu.SemaphoreType.DMA((len(operands),)),
        ],
        compiler_params=pltpu.CompilerParams(
            collective_id=0, has_side_effects=True, vmem_limit_bytes=40 * 2**20
        ),
    )(*[pltpu.with_memory_space_constraint(x, pltpu.HBM) for x in operands])
    return jnp.transpose(result, (1, 0, 2))


def solution(mesh):
    return jax.shard_map(
        shards,
        mesh=mesh,
        in_specs=(
            P(("elem", "grp"), None, None),
            P(("elem", "grp")),
            P(("elem", "grp")),
            P(),
            P(("elem", "grp"), None, None),
            P(("elem", "grp"), None),
            P(("elem", "grp"), None),
        ),
        out_specs=P(("elem", "grp"), None, None),
        check_vma=False,
    )
```
